32 devices in a mesh: groups: 2 (over y), chan: 4 (over z), tile: 2 (over x), rep: 2 (over core).
Axes of the slice: x: 2, y: 2, z: 4, core: 2. Of those that a mesh axis runs over, the one named last changes fastest.
Arguments:
- generator: float32 [8, 4, 512, 512], P(('groups', 'chan'), ('tile', 'rep')), parts along dimension 0, may hold values from -1.2 to 1.2
- hamiltonian: float32 [8, 4, 512, 512], P(('groups', 'chan'), ('tile', 'rep')), parts along dimension 0, may hold values from -1.2 to 1.2
- pair_weights: float32 [8, 4, 512], P(('groups', 'chan'), ('tile', 'rep')), parts along dimension 0, may hold values from -1 to 1
- cross_weights: float32 [8, 4, 3, 512], P(('groups', 'chan'), ('tile', 'rep')), parts along dimension 0, may hold values from -1 to 1
- recoupling: float32 [8, 16, 16], replicated, may hold values from -1.5 to 1.5
- cross_owner: int32 [8, 4], P('groups', ('tile', 'rep')), parts along dimension 0, may hold values from 0 to 3, as said below
- tile_order: int32 [8, 4, 16], P(('groups', 'chan'), ('tile', 'rep')), parts along dimension 0, may hold values from 0 to 15, each once within a row
- recoupling_index: int32 [8, 4], P('groups', ('tile', 'rep')), parts along dimension 0, may hold values from 0 to 7
Outputs:
- commutator: float32 [8, 4, 512, 512], P(('groups', 'chan'), ('tile', 'rep')), parts along dimension 0
The draws below stay inside these ranges and needn't reach their ends.
There are 2 independent parts, one for each index of `groups`. The reference program is written for one: setup_inputs(seed, part) draws one part's arguments, and reference() takes and returns one part's arrays. A program takes and returns all parts, laid end to end along the dimension named above; an argument that names none is the same for every part. Nothing has to cross between parts.
Inputs may be any that keep to these rules, and one draw needn't show every extreme that they name: `cross_owner`: in every column no owner hosts more than 3 cross-coupled channels, and one owner hosts exactly 3. `tile_order`: each channel's list names every one of its tiles once.
All inputs are finite; a program needn't handle non-finite values.
Results may differ from the reference program's by a relative error of at most 0.0003.
Values sent between devices are 32-bit elements; how exact they have to be, the bound alone decides.
A program may use at most 64 MiB of HBM per device.

```python
import math
import jax
import jax.numpy as jnp
from jax import lax

M = 512
TS = 128
GMAX = 3
NSIX = 8
TILES = 16
KCH = 4
COLS = 4


def draw_cross_owner(key, part):

    def one_column(column_key):
        heavy_key, order_key, shuffle_key = jax.random.split(column_key, 3)
        heavy = jax.random.randint(heavy_key, (), 0, KCH).astype(jnp.int32)
        shuffled = jax.random.permutation(order_key, (KCH - 1) * GMAX)
        others = (shuffled[:KCH - GMAX] // GMAX).astype(jnp.int32)
        others = others + (others >= heavy).astype(jnp.int32)
        owners = jnp.concatenate([jnp.full((GMAX,), heavy, dtype=jnp.int32), others])
        return jax.random.permutation(shuffle_key, owners).astype(jnp.int32)
    column_keys = jax.random.split(jax.random.fold_in(key, 17), COLS)
    return jnp.transpose(jax.vmap(one_column)(column_keys)).astype(jnp.int32)


def touch_ends(drawn, key, least, top_value):
    longest = drawn.shape.index(max(drawn.shape))
    spots = []
    for shift in (0, 1):
        where = [jax.random.randint(jax.random.fold_in(key, axis), (), 0, length) for axis, length in enumerate(drawn.shape)]
        where[longest] = (where[longest] + shift) % drawn.shape[longest]
        spots.append(tuple(where))
    return drawn.at[spots[0]].set(least).at[spots[1]].set(top_value)


def shard_levels(key, dims, shards, low, largest):
    def one(dim, shards_of):
        steps = jax.random.uniform(jax.random.fold_in(jax.random.fold_in(key, 6), dim), (shards_of,), jnp.float32, low / len(shards), largest / len(shards))
        return jnp.repeat(jnp.exp(steps), dims[dim] // shards_of).reshape((-1,) + (1,) * (len(dims) - dim - 1))

    loudness = one(*shards[0])
    for cut in shards[1:]:
        loudness = loudness * one(*cut)
    return loudness


def bell_draw(stream_key, shape, scale, most, cuts=(), held_as=jnp.bfloat16):
    drawn = scale * jax.random.normal(stream_key, shape, jnp.float32)
    if cuts:
        drawn = drawn * shard_levels(stream_key, shape, cuts, -0.22, 0.18)
    return jnp.clip(drawn, -most, most).astype(held_as)


def setup_inputs(seed: int = 0, part: int = 0) -> dict:
    streams_of = jax.random.split(jax.random.key(seed), 9)
    part_splits = jax.random.split(jax.random.fold_in(streams_of[8], part), 9)
    generator = bell_draw(part_splits[0], (KCH, COLS, M, M), 0.2, 1.2, ((0, 4), (1, 4)), jnp.float32)
    hamiltonian = bell_draw(part_splits[1], (KCH, COLS, M, M), 0.2, 1.2, ((0, 4), (1, 4)), jnp.float32)
    pair_weights = jnp.clip(jax.random.uniform(part_splits[2], (KCH, COLS, M), jnp.float32, -1.0, 1.0) * shard_levels(part_splits[2], (KCH, COLS, M), ((0, 4), (1, 4)), -0.4, 0.0), -1.0, 1.0)
    cross_weights = jnp.clip(jax.random.uniform(part_splits[3], (KCH, COLS, GMAX, M), jnp.float32, -1.0, 1.0) * shard_levels(part_splits[3], (KCH, COLS, GMAX, M), ((0, 4), (1, 4)), -0.4, 0.0), -1.0, 1.0)
    recoupling = bell_draw(streams_of[4], (NSIX, TILES, TILES), 0.25, 1.5, (), jnp.float32)
    cross_owner = draw_cross_owner(jax.random.fold_in(jax.random.fold_in(streams_of[8], part), 71), part)
    tile_order = jax.vmap(lambda own: jax.random.permutation(own, TILES))(jax.random.split(part_splits[6], KCH * COLS)).reshape((KCH, COLS, TILES)).astype(jnp.int32)
    recoupling_index = touch_ends(jax.random.randint(part_splits[7], (KCH, COLS), 0, NSIX), jax.random.fold_in(part_splits[7], 1), 0, NSIX - 1).astype(jnp.int32)
    return {"generator": generator, "hamiltonian": hamiltonian, "pair_weights": pair_weights, "cross_weights": cross_weights, "recoupling": recoupling, "cross_owner": cross_owner, "tile_order": tile_order, "recoupling_index": recoupling_index}


highest = lax.Precision.HIGHEST

def to_tiles(matrix, tile_size):
    leading = matrix.shape[:-2]
    blocks = matrix.shape[-1] // tile_size
    shaped = matrix.reshape(leading + (blocks, tile_size, blocks, tile_size))
    shaped = jnp.swapaxes(shaped, -3, -2)
    return shaped.reshape(leading + (blocks * blocks, tile_size, tile_size))

def from_tiles(pieces, tile_size):
    leading = pieces.shape[:-3]
    blocks = math.isqrt(pieces.shape[-3])
    shaped = pieces.reshape(leading + (blocks, blocks, tile_size, tile_size))
    shaped = jnp.swapaxes(shaped, -3, -2)
    return shaped.reshape(leading + (blocks * tile_size, blocks * tile_size))

def bracket(left_matrix, right_matrix, weights):
    scaled = weights[..., None, :]
    left_term = jnp.matmul(left_matrix * scaled, right_matrix, precision=highest)
    right_term = jnp.matmul(right_matrix * scaled, left_matrix, precision=highest)
    return left_term - right_term

def reference(generator, hamiltonian, pair_weights, cross_weights, recoupling, cross_owner, tile_order, recoupling_index):
    channels = generator.shape[0]
    column_count = generator.shape[1]
    spread = TILES // channels
    chan_range = jnp.arange(channels, dtype=jnp.int32)
    positions = jnp.arange(TILES, dtype=jnp.int32)
    source = jnp.broadcast_to(positions[None, :] % channels, (channels, TILES))
    ordinal = chan_range[:, None] * spread + positions[None, :] // channels
    earlier = chan_range[None, :] < chan_range[:, None]

    def column(column_at):
        generator_column = lax.dynamic_index_in_dim(generator, column_at, 1, keepdims=False)
        hamilton_column = lax.dynamic_index_in_dim(hamiltonian, column_at, 1, keepdims=False)
        pair_column = lax.dynamic_index_in_dim(pair_weights, column_at, 1, keepdims=False)
        cross_column = lax.dynamic_index_in_dim(cross_weights, column_at, 1, keepdims=False)
        owners = lax.dynamic_index_in_dim(cross_owner, column_at, 1, keepdims=False)
        order_column = lax.dynamic_index_in_dim(tile_order, column_at, 1, keepdims=False)
        mixer_column = lax.dynamic_index_in_dim(recoupling_index, column_at, 1, keepdims=False)
        chosen = order_column[source, ordinal]
        generator_tiles = to_tiles(generator_column, TS)
        hamilton_tiles = to_tiles(hamilton_column, TS)
        generator_cross = generator_tiles[source, chosen]
        hamilton_cross = hamilton_tiles[source, chosen]
        mixers = recoupling[mixer_column]
        generator_mixed = jnp.einsum('gji,gixy->gjxy', mixers, generator_cross, precision=highest)
        hamilton_mixed = jnp.einsum('gji,gixy->gjxy', mixers, hamilton_cross, precision=highest)
        same_owner = owners[:, None] == owners[None, :]
        slot_of = lax.optimization_barrier(jnp.sum((same_owner & earlier).astype(jnp.int32), axis=1))
        weights_cross = cross_column[owners, slot_of]
        product = bracket(from_tiles(generator_mixed, TS), from_tiles(hamilton_mixed, TS), weights_cross)
        returned = jnp.einsum('gji,gjxy->gixy', mixers, to_tiles(product, TS), precision=highest)
        placed = jnp.zeros_like(generator_tiles).at[source, chosen].set(returned)
        direct = bracket(generator_column, hamilton_column, pair_column)
        summed = direct + from_tiles(placed, TS)
        return 0.5 * (summed + jnp.swapaxes(summed, -1, -2))
    stacked = lax.map(column, jnp.arange(column_count, dtype=jnp.int32))
    return jnp.moveaxis(stacked, 0, 1)
```

```python
import functools

import jax
import jax.numpy as jnp
from jax import lax
from jax.experimental import pallas as pl
from jax.experimental.pallas import tpu as pltpu
from jax.sharding import PartitionSpec as P

TS = 128
CHUNK = 32
SUB = 16
WIDE = 256
MESH = pl.DeviceIdType.MESH


def split(x):
    high = x.astype(jnp.bfloat16)
    return high, (x - high.astype(jnp.float32)).astype(jnp.bfloat16)


def store_factor(left, right, s, rows, cols, x, weights):
    high, low = split(x * weights)
    left[2 * s, rows, cols] = high
    left[2 * s + 1, rows, cols] = low
    high, low = split(x)
    right[2 * (1 - s), rows, cols] = high
    right[2 * (1 - s) + 1, rows, cols] = low


def bracket(left, right, out):
    order = out.shape[0]

    def part(c, carry):
        cols = pl.ds(pl.multiple_of(c * WIDE, WIDE), WIDE)
        total = None
        for at_left, at_right in ((0, 0), (1, 0), (0, 1), (2, 2), (3, 2), (2, 3)):
            term = jnp.dot(
                left[at_left], right[at_right, :, cols], preferred_element_type=jnp.float32
            )
            total = term if total is None else total + term
        out[:, cols] = total
        return carry

    lax.fori_loop(0, order // WIDE, part, 0)


def kernel(
    n,
    generator,
    hamiltonian,
    pair_weights,
    cross_weights,
    recoupling,
    cross_owner,
    tile_order,
    recoupling_index,
    out,
    generator_tiles,
    hamilton_tiles,
    send,
    recv,
    weights_send,
    weights_recv,
    left,
    right,
    product,
    direct,
    back_send,
    back,
    back_turned,
    inverse,
    send_sem,
    recv_sem,
    weights_send_sem,
    weights_recv_sem,
    back_send_sem,
    back_recv_sem,
):
    me = lax.axis_index("chan")
    order = generator.shape[-1]
    blocks = order // TS
    tiles = tile_order.shape[-1]
    spread = tiles // n
    chunks = TS // CHUNK
    hosted = cross_weights.shape[2]

    def partner(d):
        p, bit = me, 1
        while bit <= d:
            if d & bit:
                p = p + bit * (1 - 2 * lax.rem(lax.div(me, bit), 2))
            bit *= 2
        return p

    distances = sorted(range(1, n), key=lambda d: -d.bit_length())
    partners = {d: partner(d) for d in range(1, n)}

    barrier = pltpu.get_barrier_semaphore()
    for d in distances:
        pl.semaphore_signal(barrier, inc=1, device_id={"chan": partners[d]}, device_id_type=MESH)

    for slot in range(hosted):
        weights_send[slot] = cross_weights[0, 0, slot : slot + 1, :]
    weights_recv[me] = weights_send[...]
    for q in range(tiles):
        here, there = pl.ds((q // blocks) * TS, TS), pl.ds((q % blocks) * TS, TS)
        generator_tiles[q] = generator[0, 0, here, there]
        hamilton_tiles[q] = hamiltonian[0, 0, here, there]

    def pack(ch, target, slot):
        for r in range(spread):
            q = tile_order[0, 0, target * spread + r]
            rows = pl.ds(pl.multiple_of(ch * CHUNK, CHUNK), CHUNK)
            slot[0, r] = generator_tiles[q, rows, :]
            slot[1, r] = hamilton_tiles[q, rows, :]

    def weights_copy(d, at):
        return pltpu.make_async_remote_copy(
            src_ref=weights_send,
            dst_ref=weights_recv.at[at],
            send_sem=weights_send_sem.at[d],
            recv_sem=weights_recv_sem.at[d],
            device_id={"chan": partners[d]},
            device_id_type=MESH,
        )

    def tiles_copy(ch, d, at):
        return pltpu.make_async_remote_copy(
            src_ref=send.at[ch, d],
            dst_ref=recv.at[ch, at],
            send_sem=send_sem.at[ch, d],
            recv_sem=recv_sem.at[ch, d],
            device_id={"chan": partners[d]},
            device_id_type=MESH,
        )

    def back_copy(d, at):
        return pltpu.make_async_remote_copy(
            src_ref=back_send.at[d],
            dst_ref=back.at[at],
            send_sem=back_send_sem.at[d],
            recv_sem=back_recv_sem.at[d],
            device_id={"chan": partners[d]},
            device_id_type=MESH,
        )

    def pack_partners(ch, carry):
        for d in distances:
            pack(ch, partners[d], send.at[ch, d])
        return carry

    def start_chunk(ch, carry):
        for d in distances:
            tiles_copy(ch, d, me).start()
        return carry

    pack_partners(0, 0)
    pl.semaphore_wait(barrier, n - 1)
    for d in distances:
        weights_copy(d, me).start()
    start_chunk(0, 0)

    def pack_and_start(ch, carry):
        pack_partners(ch, 0)
        return start_chunk(ch, carry)

    lax.fori_loop(1, chunks, pack_and_start, 0)

    def pack_own(ch, carry):
        pack(ch, me, recv.at[ch, me])
        return carry

    lax.fori_loop(0, chunks, pack_own, 0)

    pair_row = pair_weights[0]

    def split_direct(step, carry):
        rows = pl.ds(pl.multiple_of(step * SUB, SUB), SUB)
        every = slice(None)
        store_factor(left, right, 0, rows, every, generator[0, 0, rows, :], pair_row)
        store_factor(left, right, 1, rows, every, hamiltonian[0, 0, rows, :], -pair_row)
        return carry

    lax.fori_loop(0, order // SUB, split_direct, 0)
    bracket(left, right, product)
    for a in range(blocks):
        for b in range(blocks):
            here, there = pl.ds(a * TS, TS), pl.ds(b * TS, TS)
            direct[here, there] = 0.5 * (product[here, there] + product[there, here].T)

    def invert(q, carry):
        at = jnp.int32(0)
        for t in range(tiles):
            at = jnp.maximum(at, jnp.where(tile_order[0, 0, t] == q, t, 0))
        inverse[q] = at
        return carry

    lax.fori_loop(0, tiles, invert, 0)

    owner = cross_owner[me, 0]
    slot_at = jnp.int32(0)
    for g in range(n):
        slot_at = slot_at + jnp.where(
            jnp.logical_and(g < me, cross_owner[g, 0] == owner), 1, 0
        )
    slot_at = jnp.minimum(slot_at, hosted - 1)
    for d in distances:
        weights_copy(d, partners[d]).wait_recv()
    cross_row = weights_recv[owner, slot_at]
    matrix = recoupling_index[me, 0]

    def mix_chunk(ch, carry):
        for d in distances:
            tiles_copy(ch, d, partners[d]).wait_recv()

        def mix(step, inner):
            s, part = lax.div(step, CHUNK // SUB), lax.rem(step, CHUNK // SUB)
            rows = pl.ds(pl.multiple_of(part * SUB, SUB), SUB)
            signed = cross_row * (1 - 2 * s).astype(jnp.float32)
            taken = [recv[ch, i % n, s, i // n, rows, :] for i in range(tiles)]
            for j in range(tiles):
                total = taken[0] * recoupling[matrix, j, 0]
                for i in range(1, tiles):
                    total = total + taken[i] * recoupling[matrix, j, i]
                start = (j // blocks) * TS + ch * CHUNK + part * SUB
                to_rows = pl.ds(pl.multiple_of(start, SUB), SUB)
                cols = slice((j % blocks) * TS, (j % blocks + 1) * TS)
                store_factor(left, right, s, to_rows, cols, total, signed[:, cols])
            return inner

        return lax.fori_loop(0, 2 * (CHUNK // SUB), mix, carry)

    lax.fori_loop(0, chunks, mix_chunk, 0)
    bracket(left, right, product)

    def mix_back(home, slot):
        def part(c, carry):
            rows = pl.ds(pl.multiple_of(c * CHUNK, CHUNK), CHUNK)
            totals = [None] * spread
            for j in range(tiles):
                start = (j // blocks) * TS + c * CHUNK
                from_rows = pl.ds(pl.multiple_of(start, CHUNK), CHUNK)
                piece = product[from_rows, (j % blocks) * TS : (j % blocks + 1) * TS]
                for r in range(spread):
                    term = piece * recoupling[matrix, j, r * n + home]
                    totals[r] = term if j == 0 else totals[r] + term
            for r in range(spread):
                slot[r, rows, :] = totals[r]
            return carry

        lax.fori_loop(0, chunks, part, 0)

    for d in distances:
        mix_back(partners[d], back_send.at[d])
        back_copy(d, me).start()
    mix_back(me, back.at[me])

    def turn(source):
        for r in range(spread):
            back_turned[source, r] = back[source, r].T

    turn(me)
    for d in reversed(distances):
        back_copy(d, partners[d]).wait_recv()
        turn(partners[d])

    for q in range(tiles):
        a, b = q // blocks, q % blocks
        at, turned_at = inverse[q], inverse[b * blocks + a]
        came = back[lax.div(at, spread), lax.rem(at, spread)]
        turned = back_turned[lax.div(turned_at, spread), lax.rem(turned_at, spread)]
        here, there = pl.ds(a * TS, TS), pl.ds(b * TS, TS)
        out[0, 0, here, there] = direct[here, there] + 0.5 * (came + turned)

    for d in distances:
        weights_copy(d, me).wait_send()
        back_copy(d, me).wait_send()

    def finish(ch, carry):
        for d in distances:
            tiles_copy(ch, d, me).wait_send()
        return carry

    lax.fori_loop(0, chunks, finish, 0)


def solution(mesh):
    n = mesh.shape["chan"]
    placed = (
        P(("groups", "chan"), ("tile", "rep"), None, None),
        P(("groups", "chan"), ("tile", "rep"), None, None),
        P(("groups", "chan"), ("tile", "rep"), None),
        P(("groups", "chan"), ("tile", "rep"), None, None),
        P(),
        P("groups", ("tile", "rep")),
        P(("groups", "chan"), ("tile", "rep"), None),
        P("groups", ("tile", "rep")),
    )

    def body(
        generator,
        hamiltonian,
        pair_weights,
        cross_weights,
        recoupling,
        cross_owner,
        tile_order,
        recoupling_index,
    ):
        order = generator.shape[-1]
        tiles = tile_order.shape[-1]
        spread = tiles // n
        chunks = TS // CHUNK
        hosted = cross_weights.shape[2]
        f32, bf16 = jnp.float32, jnp.bfloat16
        vmem = pl.BlockSpec(memory_space=pltpu.VMEM)
        smem = pl.BlockSpec(memory_space=pltpu.SMEM)
        return pl.pallas_call(
            functools.partial(kernel, n),
            out_shape=jax.ShapeDtypeStruct(generator.shape, f32),
            in_specs=[vmem] * 4 + [smem] * 4,
            out_specs=vmem,
            scratch_shapes=[
                pltpu.VMEM((tiles, TS, TS), f32),
                pltpu.VMEM((tiles, TS, TS), f32),
                pltpu.VMEM((chunks, n, 2, spread, CHUNK, TS), f32),
                pltpu.VMEM((chunks, n, 2, spread, CHUNK, TS), f32),
                pltpu.VMEM((hosted, 1, order), f32),
                pltpu.VMEM((n, hosted, 1, order), f32),
                pltpu.VMEM((4, order, order), bf16),
                pltpu.VMEM((4, order, order), bf16),
                pltpu.VMEM((order, order), f32),
                pltpu.VMEM((order, order), f32),
                pltpu.VMEM((n, spread, TS, TS), f32),
                pltpu.VMEM((n, spread, TS, TS), f32),
                pltpu.VMEM((n, spread, TS, TS), f32),
                pltpu.SMEM((tiles,), jnp.int32),
                pltpu.SemaphoreType.DMA((chunks, n)),
                pltpu.SemaphoreType.DMA((chunks, n)),
                pltpu.SemaphoreType.DMA((n,)),
                pltpu.SemaphoreType.DMA((n,)),
                pltpu.SemaphoreType.DMA((n,)),
                pltpu.SemaphoreType.DMA((n,)),
            ],
            compiler_params=pltpu.CompilerParams(
                collective_id=0, has_side_effects=True, vmem_limit_bytes=48 * 1024 * 1024
            ),
        )(
            generator,
            hamiltonian,
            pair_weights,
            cross_weights,
            recoupling,
            cross_owner,
            tile_order,
            recoupling_index,
        )

    return jax.shard_map(
        body,
        mesh=mesh,
        in_specs=placed,
        out_specs=P(("groups", "chan"), ("tile", "rep"), None, None),
        check_vma=False,
    )
```

```python
import functools

import jax
import jax.numpy as jnp
from jax import lax
from jax.experimental import pallas as pl
from jax.experimental.pallas import tpu as pltpu
from jax.sharding import PartitionSpec as P

TS = 128
CHUNK = 32
SUB = 16
WIDE = 256
MESH = pl.DeviceIdType.MESH


def split(x):
    high = x.astype(jnp.bfloat16)
    return high, (x - high.astype(jnp.float32)).astype(jnp.bfloat16)


def store_factor(left, right, s, rows, cols, x, weights):
    high, low = split(x * weights)
    left[2 * s, rows, cols] = high
    left[2 * s + 1, rows, cols] = low
    high, low = split(x)
    right[2 * (1 - s), rows, cols] = high
    right[2 * (1 - s) + 1, rows, cols] = low


def bracket(left, right, out):
    order = out.shape[0]

    def part(c, carry):
        cols = pl.ds(pl.multiple_of(c * WIDE, WIDE), WIDE)
        total = None
        for at_left, at_right in ((0, 0), (1, 0), (0, 1), (2, 2), (3, 2), (2, 3)):
            term = jnp.dot(
                left[at_left], right[at_right, :, cols], preferred_element_type=jnp.float32
            )
            total = term if total is None else total + term
        out[:, cols] = total
        return carry

    lax.fori_loop(0, order // WIDE, part, 0)


def kernel(
    n,
    generator,
    hamiltonian,
    pair_weights_far,
    cross_weights,
    recoupling_far,
    cross_owner_far,
    tile_order_far,
    recoupling_index_far,
    out,
    generator_tiles,
    hamilton_tiles,
    pair_weights,
    recoupling,
    cross_owner,
    tile_order,
    recoupling_index,
    send,
    recv,
    weights_send,
    weights_recv,
    left,
    right,
    product,
    direct,
    back_send,
    back,
    back_turned,
    inverse,
    result,
    send_sem,
    recv_sem,
    weights_send_sem,
    weights_recv_sem,
    back_send_sem,
    back_recv_sem,
    tile_sem,
    small_sem,
):
    me = lax.axis_index("chan")
    order = generator.shape[-1]
    blocks = order // TS
    tiles = tile_order.shape[-1]
    spread = tiles // n
    chunks = TS // CHUNK
    hosted = cross_weights.shape[1]

    def partner(d):
        p, bit = me, 1
        while bit <= d:
            if d & bit:
                p = p + bit * (1 - 2 * lax.rem(lax.div(me, bit), 2))
            bit *= 2
        return p

    distances = sorted(range(1, n), key=lambda d: -d.bit_length())
    partners = {d: partner(d) for d in range(1, n)}

    barrier = pltpu.get_barrier_semaphore()
    for d in distances:
        pl.semaphore_signal(barrier, inc=1, device_id={"chan": partners[d]}, device_id_type=MESH)

    small_pairs = (
        (tile_order_far, tile_order),
        (cross_owner_far, cross_owner),
        (recoupling_index_far, recoupling_index),
        (cross_weights.at[0], weights_send),
        (pair_weights_far, pair_weights),
        (recoupling_far, recoupling),
    )
    fetches = [
        pltpu.make_async_copy(far, near, small_sem.at[at])
        for at, (far, near) in enumerate(small_pairs)
    ]
    fetches[0].start()
    for q in range(tiles):
        here, there = pl.ds((q // blocks) * TS, TS), pl.ds((q % blocks) * TS, TS)
        for s, (far, near) in enumerate(
            ((generator, generator_tiles), (hamiltonian, hamilton_tiles))
        ):
            fetch = pltpu.make_async_copy(
                far.at[0, 0, here, there], near.at[q], tile_sem.at[s, q]
            )
            fetch.start()
            fetches.append(fetch)
    for fetch in fetches[1 : len(small_pairs)]:
        fetch.start()
    for fetch in fetches:
        fetch.wait()
    weights_recv[me] = weights_send[...]

    def pack(ch, target, slot):
        for r in range(spread):
            q = tile_order[0, 0, target * spread + r]
            rows = pl.ds(pl.multiple_of(ch * CHUNK, CHUNK), CHUNK)
            slot[0, r] = generator_tiles[q, rows, :]
            slot[1, r] = hamilton_tiles[q, rows, :]

    def weights_copy(d, at):
        return pltpu.make_async_remote_copy(
            src_ref=weights_send,
            dst_ref=weights_recv.at[at],
            send_sem=weights_send_sem.at[d],
            recv_sem=weights_recv_sem.at[d],
            device_id={"chan": partners[d]},
            device_id_type=MESH,
        )

    def tiles_copy(ch, d, at):
        return pltpu.make_async_remote_copy(
            src_ref=send.at[ch, d],
            dst_ref=recv.at[ch, at],
            send_sem=send_sem.at[ch, d],
            recv_sem=recv_sem.at[ch, d],
            device_id={"chan": partners[d]},
            device_id_type=MESH,
        )

    def back_copy(d, at):
        return pltpu.make_async_remote_copy(
            src_ref=back_send.at[d],
            dst_ref=back.at[at],
            send_sem=back_send_sem.at[d],
            recv_sem=back_recv_sem.at[d],
            device_id={"chan": partners[d]},
            device_id_type=MESH,
        )

    def pack_partners(ch, carry):
        for d in distances:
            pack(ch, partners[d], send.at[ch, d])
        return carry

    def start_chunk(ch, carry):
        for d in distances:
            tiles_copy(ch, d, me).start()
        return carry

    pack_partners(0, 0)
    pl.semaphore_wait(barrier, n - 1)
    for d in distances:
        weights_copy(d, me).start()
    start_chunk(0, 0)

    def pack_and_start(ch, carry):
        pack_partners(ch, 0)
        return start_chunk(ch, carry)

    lax.fori_loop(1, chunks, pack_and_start, 0)

    def pack_own(ch, carry):
        pack(ch, me, recv.at[ch, me])
        return carry

    lax.fori_loop(0, chunks, pack_own, 0)

    pair_row = pair_weights[0]

    def split_direct(step, carry):
        a, part = lax.div(step, TS // SUB), lax.rem(step, TS // SUB)
        from_rows = pl.ds(pl.multiple_of(part * SUB, SUB), SUB)
        to_rows = pl.ds(pl.multiple_of(step * SUB, SUB), SUB)
        for b in range(blocks):
            cols = slice(b * TS, (b + 1) * TS)
            row = pair_row[:, cols]
            x, y = generator_tiles[a * blocks + b, from_rows], hamilton_tiles[a * blocks + b, from_rows]
            store_factor(left, right, 0, to_rows, cols, x, row)
            store_factor(left, right, 1, to_rows, cols, y, -row)
        return carry

    lax.fori_loop(0, order // SUB, split_direct, 0)
    bracket(left, right, product)
    for a in range(blocks):
        for b in range(blocks):
            here, there = pl.ds(a * TS, TS), pl.ds(b * TS, TS)
            direct[here, there] = 0.5 * (product[here, there] + product[there, here].T)

    def invert(q, carry):
        at = jnp.int32(0)
        for t in range(tiles):
            at = jnp.maximum(at, jnp.where(tile_order[0, 0, t] == q, t, 0))
        inverse[q] = at
        return carry

    lax.fori_loop(0, tiles, invert, 0)

    owner = cross_owner[0, me]
    slot_at = jnp.int32(0)
    for g in range(n):
        slot_at = slot_at + jnp.where(
            jnp.logical_and(g < me, cross_owner[0, g] == owner), 1, 0
        )
    slot_at = jnp.minimum(slot_at, hosted - 1)
    for d in distances:
        weights_copy(d, partners[d]).wait_recv()
    cross_row = weights_recv[owner, slot_at]
    matrix = recoupling_index[0, me]

    def mix_chunk(ch, carry):
        for d in distances:
            tiles_copy(ch, d, partners[d]).wait_recv()

        def mix(step, inner):
            s, part = lax.div(step, CHUNK // SUB), lax.rem(step, CHUNK // SUB)
            rows = pl.ds(pl.multiple_of(part * SUB, SUB), SUB)
            signed = cross_row * (1 - 2 * s).astype(jnp.float32)
            taken = [recv[ch, i % n, s, i // n, rows, :] for i in range(tiles)]
            for j in range(tiles):
                total = taken[0] * recoupling[matrix, j, 0]
                for i in range(1, tiles):
                    total = total + taken[i] * recoupling[matrix, j, i]
                start = (j // blocks) * TS + ch * CHUNK + part * SUB
                to_rows = pl.ds(pl.multiple_of(start, SUB), SUB)
                cols = slice((j % blocks) * TS, (j % blocks + 1) * TS)
                store_factor(left, right, s, to_rows, cols, total, signed[:, cols])
            return inner

        return lax.fori_loop(0, 2 * (CHUNK // SUB), mix, carry)

    lax.fori_loop(0, chunks, mix_chunk, 0)
    bracket(left, right, product)

    def mix_back(home, slot):
        def part(c, carry):
            rows = pl.ds(pl.multiple_of(c * CHUNK, CHUNK), CHUNK)
            totals = [None] * spread
            for j in range(tiles):
                start = (j // blocks) * TS + c * CHUNK
                from_rows = pl.ds(pl.multiple_of(start, CHUNK), CHUNK)
                piece = product[from_rows, (j % blocks) * TS : (j % blocks + 1) * TS]
                for r in range(spread):
                    term = piece * recoupling[matrix, j, r * n + home]
                    totals[r] = term if j == 0 else totals[r] + term
            for r in range(spread):
                slot[r, rows, :] = totals[r]
            return carry

        lax.fori_loop(0, chunks, part, 0)

    for d in distances:
        mix_back(partners[d], back_send.at[d])
        back_copy(d, me).start()
    mix_back(me, back.at[me])

    def turn(source):
        for r in range(spread):
            back_turned[source, r] = back[source, r].T

    turn(me)
    for d in reversed(distances):
        back_copy(d, partners[d]).wait_recv()
        turn(partners[d])

    writes = []
    for q in range(tiles):
        a, b = q // blocks, q % blocks
        at, turned_at = inverse[q], inverse[b * blocks + a]
        came = back[lax.div(at, spread), lax.rem(at, spread)]
        turned = back_turned[lax.div(turned_at, spread), lax.rem(turned_at, spread)]
        here, there = pl.ds(a * TS, TS), pl.ds(b * TS, TS)
        result[q] = direct[here, there] + 0.5 * (came + turned)
        write = pltpu.make_async_copy(result.at[q], out.at[0, 0, here, there], tile_sem.at[0, q])
        write.start()
        writes.append(write)

    for d in distances:
        weights_copy(d, me).wait_send()
        back_copy(d, me).wait_send()

    def finish(ch, carry):
        for d in distances:
            tiles_copy(ch, d, me).wait_send()
        return carry

    lax.fori_loop(0, chunks, finish, 0)
    for write in writes:
        write.wait()


def solution(mesh):
    n = mesh.shape["chan"]
    placed = (
        P(("groups", "chan"), ("tile", "rep"), None, None),
        P(("groups", "chan"), ("tile", "rep"), None, None),
        P(("groups", "chan"), ("tile", "rep"), None),
        P(("groups", "chan"), ("tile", "rep"), None, None),
        P(),
        P("groups", ("tile", "rep")),
        P(("groups", "chan"), ("tile", "rep"), None),
        P("groups", ("tile", "rep")),
    )

    def body(
        generator,
        hamiltonian,
        pair_weights,
        cross_weights,
        recoupling,
        cross_owner,
        tile_order,
        recoupling_index,
    ):
        order = generator.shape[-1]
        tiles = tile_order.shape[-1]
        spread = tiles // n
        chunks = TS // CHUNK
        hosted = cross_weights.shape[2]
        f32, bf16 = jnp.float32, jnp.bfloat16
        return pl.pallas_call(
            functools.partial(kernel, n),
            out_shape=jax.ShapeDtypeStruct(generator.shape, f32),
            in_specs=[pl.BlockSpec(memory_space=pltpu.HBM)] * 8,
            out_specs=pl.BlockSpec(memory_space=pltpu.HBM),
            scratch_shapes=[
                pltpu.VMEM((tiles, TS, TS), f32),
                pltpu.VMEM((tiles, TS, TS), f32),
                pltpu.VMEM(pair_weights.shape, f32),
                pltpu.SMEM(recoupling.shape, f32),
                pltpu.SMEM((1, n), jnp.int32),
                pltpu.SMEM(tile_order.shape, jnp.int32),
                pltpu.SMEM((1, n), jnp.int32),
                pltpu.VMEM((chunks, n, 2, spread, CHUNK, TS), f32),
                pltpu.VMEM((chunks, n, 2, spread, CHUNK, TS), f32),
                pltpu.VMEM((hosted, 1, order), f32),
                pltpu.VMEM((n, hosted, 1, order), f32),
                pltpu.VMEM((4, order, order), bf16),
                pltpu.VMEM((4, order, order), bf16),
                pltpu.VMEM((order, order), f32),
                pltpu.VMEM((order, order), f32),
                pltpu.VMEM((n, spread, TS, TS), f32),
                pltpu.VMEM((n, spread, TS, TS), f32),
                pltpu.VMEM((n, spread, TS, TS), f32),
                pltpu.SMEM((tiles,), jnp.int32),
                pltpu.VMEM((tiles, TS, TS), f32),
                pltpu.SemaphoreType.DMA((chunks, n)),
                pltpu.SemaphoreType.DMA((chunks, n)),
                pltpu.SemaphoreType.DMA((n,)),
                pltpu.SemaphoreType.DMA((n,)),
                pltpu.SemaphoreType.DMA((n,)),
                pltpu.SemaphoreType.DMA((n,)),
                pltpu.SemaphoreType.DMA((2, tiles)),
                pltpu.SemaphoreType.DMA((6,)),
            ],
            compiler_params=pltpu.CompilerParams(
                collective_id=0, has_side_effects=True, vmem_limit_bytes=64 * 1024 * 1024
            ),
        )(
            generator,
            hamiltonian,
            pair_weights,
            jnp.swapaxes(cross_weights, 1, 2),
            recoupling,
            jnp.transpose(cross_owner),
            tile_order,
            jnp.transpose(recoupling_index),
        )

    return jax.shard_map(
        body,
        mesh=mesh,
        in_specs=placed,
        out_specs=P(("groups", "chan"), ("tile", "rep"), None, None),
        check_vma=False,
    )
```

```python
import functools

import jax
import jax.numpy as jnp
from jax import lax
from jax.experimental import pallas as pl
from jax.experimental.pallas import tpu as pltpu
from jax.sharding import PartitionSpec as P

TS = 128
CHUNK = 32
SUB = 16
WIDE = 256
MESH = pl.DeviceIdType.MESH


def split(x):
    high = x.astype(jnp.bfloat16)
    return high, (x - high.astype(jnp.float32)).astype(jnp.bfloat16)


def store_factor(left, right, s, rows, cols, x, weights):
    high, low = split(x * weights)
    left[2 * s, rows, cols] = high
    left[2 * s + 1, rows, cols] = low
    high, low = split(x)
    right[2 * (1 - s), rows, cols] = high
    right[2 * (1 - s) + 1, rows, cols] = low


def bracket(left, right, out):
    order = out.shape[0]

    def part(c, carry):
        cols = pl.ds(pl.multiple_of(c * WIDE, WIDE), WIDE)
        total = None
        for at_left, at_right in ((0, 0), (1, 0), (0, 1), (2, 2), (3, 2), (2, 3)):
            term = jnp.dot(
                left[at_left], right[at_right, :, cols], preferred_element_type=jnp.float32
            )
            total = term if total is None else total + term
        out[:, cols] = total
        return carry

    lax.fori_loop(0, order // WIDE, part, 0)


def kernel(
    n,
    generator,
    hamiltonian,
    pair_weights_far,
    cross_weights,
    recoupling_far,
    cross_owner_far,
    tile_order_far,
    recoupling_index_far,
    out,
    generator_tiles,
    hamilton_tiles,
    pair_weights,
    recoupling,
    cross_owner,
    tile_order,
    recoupling_index,
    send,
    recv,
    weights_send,
    weights_recv,
    left,
    right,
    product,
    direct,
    back_send,
    back,
    back_turned,
    inverse,
    result,
    send_sem,
    recv_sem,
    weights_send_sem,
    weights_recv_sem,
    back_send_sem,
    back_recv_sem,
    tile_sem,
    small_sem,
):
    me = lax.axis_index("chan")
    order = generator.shape[-1]
    blocks = order // TS
    tiles = tile_order.shape[-1]
    spread = tiles // n
    chunks = TS // CHUNK
    hosted = cross_weights.shape[1]

    def partner(d):
        p, bit = me, 1
        while bit <= d:
            if d & bit:
                p = p + bit * (1 - 2 * lax.rem(lax.div(me, bit), 2))
            bit *= 2
        return p

    distances = sorted(range(1, n), key=lambda d: -d.bit_length())
    partners = {d: partner(d) for d in range(1, n)}

    barrier = pltpu.get_barrier_semaphore()
    for d in distances:
        pl.semaphore_signal(barrier, inc=1, device_id={"chan": partners[d]}, device_id_type=MESH)

    small_pairs = (
        (tile_order_far, tile_order),
        (cross_owner_far, cross_owner),
        (recoupling_index_far, recoupling_index),
        (cross_weights.at[0], weights_send),
        (pair_weights_far, pair_weights),
        (recoupling_far, recoupling),
    )
    fetches = [
        pltpu.make_async_copy(far, near, small_sem.at[at])
        for at, (far, near) in enumerate(small_pairs)
    ]
    fetches[0].start()
    for q in range(tiles):
        here, there = pl.ds((q // blocks) * TS, TS), pl.ds((q % blocks) * TS, TS)
        for s, (far, near) in enumerate(
            ((generator, generator_tiles), (hamiltonian, hamilton_tiles))
        ):
            fetch = pltpu.make_async_copy(
                far.at[0, 0, here, there], near.at[q], tile_sem.at[s, q]
            )
            fetch.start()
            fetches.append(fetch)
    for fetch in fetches[1 : len(small_pairs)]:
        fetch.start()
    for fetch in fetches:
        fetch.wait()
    weights_recv[me] = weights_send[...]

    def pack(ch, target, slot):
        for r in range(spread):
            q = tile_order[0, 0, target * spread + r]
            rows = pl.ds(pl.multiple_of(ch * CHUNK, CHUNK), CHUNK)
            slot[0, r] = generator_tiles[q, rows, :]
            slot[1, r] = hamilton_tiles[q, rows, :]

    def weights_copy(d, at):
        return pltpu.make_async_remote_copy(
            src_ref=weights_send,
            dst_ref=weights_recv.at[at],
            send_sem=weights_send_sem.at[d],
            recv_sem=weights_recv_sem.at[d],
            device_id={"chan": partners[d]},
            device_id_type=MESH,
        )

    def tiles_copy(ch, d, at):
        return pltpu.make_async_remote_copy(
            src_ref=send.at[ch, d],
            dst_ref=recv.at[ch, at],
            send_sem=send_sem.at[ch, d],
            recv_sem=recv_sem.at[ch, d],
            device_id={"chan": partners[d]},
            device_id_type=MESH,
        )

    def back_copy(d, at):
        return pltpu.make_async_remote_copy(
            src_ref=back_send.at[d],
            dst_ref=back.at[at],
            send_sem=back_send_sem.at[d],
            recv_sem=back_recv_sem.at[d],
            device_id={"chan": partners[d]},
            device_id_type=MESH,
        )

    def pack_partners(ch, carry):
        for d in distances:
            pack(ch, partners[d], send.at[ch, d])
        return carry

    def start_chunk(ch, carry):
        for d in distances:
            tiles_copy(ch, d, me).start()
        return carry

    def pack_and_start(ch, carry):
        pack_partners(ch, 0)
        return start_chunk(ch, carry)

    first = lax.axis_index("rep") == 0
    pack_partners(0, 0)
    pl.semaphore_wait(barrier, n - 1)
    for d in distances:
        weights_copy(d, me).start()

    @pl.when(first)
    def _():
        start_chunk(0, 0)
        lax.fori_loop(1, chunks, pack_and_start, 0)

    def pack_own(ch, carry):
        pack(ch, me, recv.at[ch, me])
        return carry

    lax.fori_loop(0, chunks, pack_own, 0)

    pair_row = pair_weights[0]

    def split_direct(step, carry):
        a, part = lax.div(step, TS // SUB), lax.rem(step, TS // SUB)
        from_rows = pl.ds(pl.multiple_of(part * SUB, SUB), SUB)
        to_rows = pl.ds(pl.multiple_of(step * SUB, SUB), SUB)
        for b in range(blocks):
            cols = slice(b * TS, (b + 1) * TS)
            row = pair_row[:, cols]
            x, y = generator_tiles[a * blocks + b, from_rows], hamilton_tiles[a * blocks + b, from_rows]
            store_factor(left, right, 0, to_rows, cols, x, row)
            store_factor(left, right, 1, to_rows, cols, y, -row)
        return carry

    lax.fori_loop(0, order // SUB, split_direct, 0)
    bracket(left, right, product)

    @pl.when(jnp.logical_not(first))
    def _():
        start_chunk(0, 0)
        lax.fori_loop(1, chunks, pack_and_start, 0)

    for a in range(blocks):
        for b in range(blocks):
            here, there = pl.ds(a * TS, TS), pl.ds(b * TS, TS)
            direct[here, there] = 0.5 * (product[here, there] + product[there, here].T)

    def invert(q, carry):
        at = jnp.int32(0)
        for t in range(tiles):
            at = jnp.maximum(at, jnp.where(tile_order[0, 0, t] == q, t, 0))
        inverse[q] = at
        return carry

    lax.fori_loop(0, tiles, invert, 0)

    owner = cross_owner[0, me]
    slot_at = jnp.int32(0)
    for g in range(n):
        slot_at = slot_at + jnp.where(
            jnp.logical_and(g < me, cross_owner[0, g] == owner), 1, 0
        )
    slot_at = jnp.minimum(slot_at, hosted - 1)
    for d in distances:
        weights_copy(d, partners[d]).wait_recv()
    cross_row = weights_recv[owner, slot_at]
    matrix = recoupling_index[0, me]

    def mix_chunk(ch, carry):
        for d in distances:
            tiles_copy(ch, d, partners[d]).wait_recv()

        def mix(step, inner):
            s, part = lax.div(step, CHUNK // SUB), lax.rem(step, CHUNK // SUB)
            rows = pl.ds(pl.multiple_of(part * SUB, SUB), SUB)
            signed = cross_row * (1 - 2 * s).astype(jnp.float32)
            taken = [recv[ch, i % n, s, i // n, rows, :] for i in range(tiles)]
            for j in range(tiles):
                total = taken[0] * recoupling[matrix, j, 0]
                for i in range(1, tiles):
                    total = total + taken[i] * recoupling[matrix, j, i]
                start = (j // blocks) * TS + ch * CHUNK + part * SUB
                to_rows = pl.ds(pl.multiple_of(start, SUB), SUB)
                cols = slice((j % blocks) * TS, (j % blocks + 1) * TS)
                store_factor(left, right, s, to_rows, cols, total, signed[:, cols])
            return inner

        return lax.fori_loop(0, 2 * (CHUNK // SUB), mix, carry)

    lax.fori_loop(0, chunks, mix_chunk, 0)
    bracket(left, right, product)

    def mix_back(home, slot):
        def part(c, carry):
            rows = pl.ds(pl.multiple_of(c * CHUNK, CHUNK), CHUNK)
            totals = [None] * spread
            for j in range(tiles):
                start = (j // blocks) * TS + c * CHUNK
                from_rows = pl.ds(pl.multiple_of(start, CHUNK), CHUNK)
                piece = product[from_rows, (j % blocks) * TS : (j % blocks + 1) * TS]
                for r in range(spread):
                    term = piece * recoupling[matrix, j, r * n + home]
                    totals[r] = term if j == 0 else totals[r] + term
            for r in range(spread):
                slot[r, rows, :] = totals[r]
            return carry

        lax.fori_loop(0, chunks, part, 0)

    for d in distances:
        mix_back(partners[d], back_send.at[d])
        back_copy(d, me).start()
    mix_back(me, back.at[me])

    def turn(source):
        for r in range(spread):
            back_turned[source, r] = back[source, r].T

    turn(me)
    for d in reversed(distances):
        back_copy(d, partners[d]).wait_recv()
        turn(partners[d])

    writes = []
    for q in range(tiles):
        a, b = q // blocks, q % blocks
        at, turned_at = inverse[q], inverse[b * blocks + a]
        came = back[lax.div(at, spread), lax.rem(at, spread)]
        turned = back_turned[lax.div(turned_at, spread), lax.rem(turned_at, spread)]
        here, there = pl.ds(a * TS, TS), pl.ds(b * TS, TS)
        result[q] = direct[here, there] + 0.5 * (came + turned)
        write = pltpu.make_async_copy(result.at[q], out.at[0, 0, here, there], tile_sem.at[0, q])
        write.start()
        writes.append(write)

    for d in distances:
        weights_copy(d, me).wait_send()
        back_copy(d, me).wait_send()

    def finish(ch, carry):
        for d in distances:
            tiles_copy(ch, d, me).wait_send()
        return carry

    lax.fori_loop(0, chunks, finish, 0)
    for write in writes:
        write.wait()


def solution(mesh):
    n = mesh.shape["chan"]
    placed = (
        P(("groups", "chan"), ("tile", "rep"), None, None),
        P(("groups", "chan"), ("tile", "rep"), None, None),
        P(("groups", "chan"), ("tile", "rep"), None),
        P(("groups", "chan"), ("tile", "rep"), None, None),
        P(),
        P("groups", ("tile", "rep")),
        P(("groups", "chan"), ("tile", "rep"), None),
        P("groups", ("tile", "rep")),
    )

    def body(
        generator,
        hamiltonian,
        pair_weights,
        cross_weights,
        recoupling,
        cross_owner,
        tile_order,
        recoupling_index,
    ):
        order = generator.shape[-1]
        tiles = tile_order.shape[-1]
        spread = tiles // n
        chunks = TS // CHUNK
        hosted = cross_weights.shape[2]
        f32, bf16 = jnp.float32, jnp.bfloat16
        return pl.pallas_call(
            functools.partial(kernel, n),
            out_shape=jax.ShapeDtypeStruct(generator.shape, f32),
            in_specs=[pl.BlockSpec(memory_space=pltpu.HBM)] * 8,
            out_specs=pl.BlockSpec(memory_space=pltpu.HBM),
            scratch_shapes=[
                pltpu.VMEM((tiles, TS, TS), f32),
                pltpu.VMEM((tiles, TS, TS), f32),
                pltpu.VMEM(pair_weights.shape, f32),
                pltpu.SMEM(recoupling.shape, f32),
                pltpu.SMEM((1, n), jnp.int32),
                pltpu.SMEM(tile_order.shape, jnp.int32),
                pltpu.SMEM((1, n), jnp.int32),
                pltpu.VMEM((chunks, n, 2, spread, CHUNK, TS), f32),
                pltpu.VMEM((chunks, n, 2, spread, CHUNK, TS), f32),
                pltpu.VMEM((hosted, 1, order), f32),
                pltpu.VMEM((n, hosted, 1, order), f32),
                pltpu.VMEM((4, order, order), bf16),
                pltpu.VMEM((4, order, order), bf16),
                pltpu.VMEM((order, order), f32),
                pltpu.VMEM((order, order), f32),
                pltpu.VMEM((n, spread, TS, TS), f32),
                pltpu.VMEM((n, spread, TS, TS), f32),
                pltpu.VMEM((n, spread, TS, TS), f32),
                pltpu.SMEM((tiles,), jnp.int32),
                pltpu.VMEM((tiles, TS, TS), f32),
                pltpu.SemaphoreType.DMA((chunks, n)),
                pltpu.SemaphoreType.DMA((chunks, n)),
                pltpu.SemaphoreType.DMA((n,)),
                pltpu.SemaphoreType.DMA((n,)),
                pltpu.SemaphoreType.DMA((n,)),
                pltpu.SemaphoreType.DMA((n,)),
                pltpu.SemaphoreType.DMA((2, tiles)),
                pltpu.SemaphoreType.DMA((6,)),
            ],
            compiler_params=pltpu.CompilerParams(
                collective_id=0, has_side_effects=True, vmem_limit_bytes=64 * 1024 * 1024
            ),
        )(
            generator,
            hamiltonian,
            pair_weights,
            jnp.swapaxes(cross_weights, 1, 2),
            recoupling,
            jnp.transpose(cross_owner),
            tile_order,
            jnp.transpose(recoupling_index),
        )

    return jax.shard_map(
        body,
        mesh=mesh,
        in_specs=placed,
        out_specs=P(("groups", "chan"), ("tile", "rep"), None, None),
        check_vma=False,
    )
```

```python
import functools

import jax
import jax.numpy as jnp
from jax import lax
from jax.experimental import pallas as pl
from jax.experimental.pallas import tpu as pltpu
from jax.sharding import PartitionSpec as P

TS = 128
CHUNK = 32
SUB = 16
WIDE = 256
MESH = pl.DeviceIdType.MESH


def split(x):
    high = x.astype(jnp.bfloat16)
    return high, (x - high.astype(jnp.float32)).astype(jnp.bfloat16)


def store_factor(left, right, s, rows, cols, x, weights):
    high, low = split(x * weights)
    left[2 * s, rows, cols] = high
    left[2 * s + 1, rows, cols] = low
    high, low = split(x)
    right[2 * (1 - s), rows, cols] = high
    right[2 * (1 - s) + 1, rows, cols] = low


def bracket(left, right, out):
    order = out.shape[0]

    def part(c, carry):
        cols = pl.ds(pl.multiple_of(c * WIDE, WIDE), WIDE)
        total = None
        for at_left, at_right in ((0, 0), (1, 0), (0, 1), (2, 2), (3, 2), (2, 3)):
            term = jnp.dot(
                left[at_left], right[at_right, :, cols], preferred_element_type=jnp.float32
            )
            total = term if total is None else total + term
        out[:, cols] = total
        return carry

    lax.fori_loop(0, order // WIDE, part, 0)


def kernel(
    n,
    generator,
    hamiltonian,
    pair_weights_far,
    cross_weights,
    recoupling_far,
    cross_owner_far,
    tile_order_far,
    recoupling_index_far,
    out,
    generator_tiles,
    hamilton_tiles,
    pair_weights,
    recoupling,
    cross_owner,
    tile_order,
    recoupling_index,
    send,
    recv,
    weights_send,
    weights_recv,
    left,
    right,
    product,
    direct,
    back_send,
    back,
    back_turned,
    inverse,
    result,
    send_sem,
    recv_sem,
    weights_send_sem,
    weights_recv_sem,
    back_send_sem,
    back_recv_sem,
    tile_sem,
    small_sem,
):
    me = lax.axis_index("chan")
    order = generator.shape[-1]
    blocks = order // TS
    tiles = tile_order.shape[-1]
    spread = tiles // n
    chunks = TS // CHUNK
    hosted = cross_weights.shape[1]

    def partner(d):
        p, bit = me, 1
        while bit <= d:
            if d & bit:
                p = p + bit * (1 - 2 * lax.rem(lax.div(me, bit), 2))
            bit *= 2
        return p

    distances = sorted(range(1, n), key=lambda d: -d.bit_length())
    first = lax.axis_index("rep") == 0

    def by_core(act):
        @pl.when(first)
        def _():
            act(list(reversed(distances)))

        @pl.when(jnp.logical_not(first))
        def _():
            act(distances)

    partners = {d: partner(d) for d in range(1, n)}

    barrier = pltpu.get_barrier_semaphore()
    for d in distances:
        pl.semaphore_signal(barrier, inc=1, device_id={"chan": partners[d]}, device_id_type=MESH)

    small_pairs = (
        (tile_order_far, tile_order),
        (cross_owner_far, cross_owner),
        (recoupling_index_far, recoupling_index),
        (cross_weights.at[0], weights_send),
        (pair_weights_far, pair_weights),
        (recoupling_far, recoupling),
    )
    fetches = [
        pltpu.make_async_copy(far, near, small_sem.at[at])
        for at, (far, near) in enumerate(small_pairs)
    ]
    fetches[0].start()
    for q in range(tiles):
        here, there = pl.ds((q // blocks) * TS, TS), pl.ds((q % blocks) * TS, TS)
        for s, (far, near) in enumerate(
            ((generator, generator_tiles), (hamiltonian, hamilton_tiles))
        ):
            fetch = pltpu.make_async_copy(
                far.at[0, 0, here, there], near.at[q], tile_sem.at[s, q]
            )
            fetch.start()
            fetches.append(fetch)
    for fetch in fetches[1 : len(small_pairs)]:
        fetch.start()
    for fetch in fetches:
        fetch.wait()
    weights_recv[me] = weights_send[...]

    def pack(ch, target, slot):
        for r in range(spread):
            q = tile_order[0, 0, target * spread + r]
            rows = pl.ds(pl.multiple_of(ch * CHUNK, CHUNK), CHUNK)
            slot[0, r] = generator_tiles[q, rows, :]
            slot[1, r] = hamilton_tiles[q, rows, :]

    def weights_copy(d, at):
        return pltpu.make_async_remote_copy(
            src_ref=weights_send,
            dst_ref=weights_recv.at[at],
            send_sem=weights_send_sem.at[d],
            recv_sem=weights_recv_sem.at[d],
            device_id={"chan": partners[d]},
            device_id_type=MESH,
        )

    def tiles_copy(ch, d, at):
        return pltpu.make_async_remote_copy(
            src_ref=send.at[ch, d],
            dst_ref=recv.at[ch, at],
            send_sem=send_sem.at[ch, d],
            recv_sem=recv_sem.at[ch, d],
            device_id={"chan": partners[d]},
            device_id_type=MESH,
        )

    def back_copy(d, at):
        return pltpu.make_async_remote_copy(
            src_ref=back_send.at[d],
            dst_ref=back.at[at],
            send_sem=back_send_sem.at[d],
            recv_sem=back_recv_sem.at[d],
            device_id={"chan": partners[d]},
            device_id_type=MESH,
        )

    def pack_partners(ch, carry):
        for d in distances:
            pack(ch, partners[d], send.at[ch, d])
        return carry

    def start_chunk(ch, carry):
        def act(ordered):
            for d in ordered:
                tiles_copy(ch, d, me).start()

        by_core(act)
        return carry

    pack_partners(0, 0)
    pl.semaphore_wait(barrier, n - 1)
    for d in distances:
        weights_copy(d, me).start()
    start_chunk(0, 0)

    def pack_and_start(ch, carry):
        pack_partners(ch, 0)
        return start_chunk(ch, carry)

    lax.fori_loop(1, chunks, pack_and_start, 0)

    def pack_own(ch, carry):
        pack(ch, me, recv.at[ch, me])
        return carry

    lax.fori_loop(0, chunks, pack_own, 0)

    pair_row = pair_weights[0]

    def split_direct(step, carry):
        a, part = lax.div(step, TS // SUB), lax.rem(step, TS // SUB)
        from_rows = pl.ds(pl.multiple_of(part * SUB, SUB), SUB)
        to_rows = pl.ds(pl.multiple_of(step * SUB, SUB), SUB)
        for b in range(blocks):
            cols = slice(b * TS, (b + 1) * TS)
            row = pair_row[:, cols]
            x, y = generator_tiles[a * blocks + b, from_rows], hamilton_tiles[a * blocks + b, from_rows]
            store_factor(left, right, 0, to_rows, cols, x, row)
            store_factor(left, right, 1, to_rows, cols, y, -row)
        return carry

    lax.fori_loop(0, order // SUB, split_direct, 0)
    bracket(left, right, product)
    for a in range(blocks):
        for b in range(blocks):
            here, there = pl.ds(a * TS, TS), pl.ds(b * TS, TS)
            direct[here, there] = 0.5 * (product[here, there] + product[there, here].T)

    def invert(q, carry):
        at = jnp.int32(0)
        for t in range(tiles):
            at = jnp.maximum(at, jnp.where(tile_order[0, 0, t] == q, t, 0))
        inverse[q] = at
        return carry

    lax.fori_loop(0, tiles, invert, 0)

    owner = cross_owner[0, me]
    slot_at = jnp.int32(0)
    for g in range(n):
        slot_at = slot_at + jnp.where(
            jnp.logical_and(g < me, cross_owner[0, g] == owner), 1, 0
        )
    slot_at = jnp.minimum(slot_at, hosted - 1)
    for d in distances:
        weights_copy(d, partners[d]).wait_recv()
    cross_row = weights_recv[owner, slot_at]
    matrix = recoupling_index[0, me]

    def mix_chunk(ch, carry):
        for d in distances:
            tiles_copy(ch, d, partners[d]).wait_recv()

        def mix(step, inner):
            s, part = lax.div(step, CHUNK // SUB), lax.rem(step, CHUNK // SUB)
            rows = pl.ds(pl.multiple_of(part * SUB, SUB), SUB)
            signed = cross_row * (1 - 2 * s).astype(jnp.float32)
            taken = [recv[ch, i % n, s, i // n, rows, :] for i in range(tiles)]
            for j in range(tiles):
                total = taken[0] * recoupling[matrix, j, 0]
                for i in range(1, tiles):
                    total = total + taken[i] * recoupling[matrix, j, i]
                start = (j // blocks) * TS + ch * CHUNK + part * SUB
                to_rows = pl.ds(pl.multiple_of(start, SUB), SUB)
                cols = slice((j % blocks) * TS, (j % blocks + 1) * TS)
                store_factor(left, right, s, to_rows, cols, total, signed[:, cols])
            return inner

        return lax.fori_loop(0, 2 * (CHUNK // SUB), mix, carry)

    lax.fori_loop(0, chunks, mix_chunk, 0)
    bracket(left, right, product)

    def mix_back(home, slot):
        def part(c, carry):
            rows = pl.ds(pl.multiple_of(c * CHUNK, CHUNK), CHUNK)
            totals = [None] * spread
            for j in range(tiles):
                start = (j // blocks) * TS + c * CHUNK
                from_rows = pl.ds(pl.multiple_of(start, CHUNK), CHUNK)
                piece = product[from_rows, (j % blocks) * TS : (j % blocks + 1) * TS]
                for r in range(spread):
                    term = piece * recoupling[matrix, j, r * n + home]
                    totals[r] = term if j == 0 else totals[r] + term
            for r in range(spread):
                slot[r, rows, :] = totals[r]
            return carry

        lax.fori_loop(0, chunks, part, 0)

    def send_back(ordered):
        for d in ordered:
            mix_back(partners[d], back_send.at[d])
            back_copy(d, me).start()

    by_core(send_back)
    mix_back(me, back.at[me])

    def turn(source):
        for r in range(spread):
            back_turned[source, r] = back[source, r].T

    turn(me)
    for d in reversed(distances):
        back_copy(d, partners[d]).wait_recv()
        turn(partners[d])

    writes = []
    for q in range(tiles):
        a, b = q // blocks, q % blocks
        at, turned_at = inverse[q], inverse[b * blocks + a]
        came = back[lax.div(at, spread), lax.rem(at, spread)]
        turned = back_turned[lax.div(turned_at, spread), lax.rem(turned_at, spread)]
        here, there = pl.ds(a * TS, TS), pl.ds(b * TS, TS)
        result[q] = direct[here, there] + 0.5 * (came + turned)
        write = pltpu.make_async_copy(result.at[q], out.at[0, 0, here, there], tile_sem.at[0, q])
        write.start()
        writes.append(write)

    for d in distances:
        weights_copy(d, me).wait_send()
        back_copy(d, me).wait_send()

    def finish(ch, carry):
        for d in distances:
            tiles_copy(ch, d, me).wait_send()
        return carry

    lax.fori_loop(0, chunks, finish, 0)
    for write in writes:
        write.wait()


def solution(mesh):
    n = mesh.shape["chan"]
    placed = (
        P(("groups", "chan"), ("tile", "rep"), None, None),
        P(("groups", "chan"), ("tile", "rep"), None, None),
        P(("groups", "chan"), ("tile", "rep"), None),
        P(("groups", "chan"), ("tile", "rep"), None, None),
        P(),
        P("groups", ("tile", "rep")),
        P(("groups", "chan"), ("tile", "rep"), None),
        P("groups", ("tile", "rep")),
    )

    def body(
        generator,
        hamiltonian,
        pair_weights,
        cross_weights,
        recoupling,
        cross_owner,
        tile_order,
        recoupling_index,
    ):
        order = generator.shape[-1]
        tiles = tile_order.shape[-1]
        spread = tiles // n
        chunks = TS // CHUNK
        hosted = cross_weights.shape[2]
        f32, bf16 = jnp.float32, jnp.bfloat16
        return pl.pallas_call(
            functools.partial(kernel, n),
            out_shape=jax.ShapeDtypeStruct(generator.shape, f32),
            in_specs=[pl.BlockSpec(memory_space=pltpu.HBM)] * 8,
            out_specs=pl.BlockSpec(memory_space=pltpu.HBM),
            scratch_shapes=[
                pltpu.VMEM((tiles, TS, TS), f32),
                pltpu.VMEM((tiles, TS, TS), f32),
                pltpu.VMEM(pair_weights.shape, f32),
                pltpu.SMEM(recoupling.shape, f32),
                pltpu.SMEM((1, n), jnp.int32),
                pltpu.SMEM(tile_order.shape, jnp.int32),
                pltpu.SMEM((1, n), jnp.int32),
                pltpu.VMEM((chunks, n, 2, spread, CHUNK, TS), f32),
                pltpu.VMEM((chunks, n, 2, spread, CHUNK, TS), f32),
                pltpu.VMEM((hosted, 1, order), f32),
                pltpu.VMEM((n, hosted, 1, order), f32),
                pltpu.VMEM((4, order, order), bf16),
                pltpu.VMEM((4, order, order), bf16),
                pltpu.VMEM((order, order), f32),
                pltpu.VMEM((order, order), f32),
                pltpu.VMEM((n, spread, TS, TS), f32),
                pltpu.VMEM((n, spread, TS, TS), f32),
                pltpu.VMEM((n, spread, TS, TS), f32),
                pltpu.SMEM((tiles,), jnp.int32),
                pltpu.VMEM((tiles, TS, TS), f32),
                pltpu.SemaphoreType.DMA((chunks, n)),
                pltpu.SemaphoreType.DMA((chunks, n)),
                pltpu.SemaphoreType.DMA((n,)),
                pltpu.SemaphoreType.DMA((n,)),
                pltpu.SemaphoreType.DMA((n,)),
                pltpu.SemaphoreType.DMA((n,)),
                pltpu.SemaphoreType.DMA((2, tiles)),
                pltpu.SemaphoreType.DMA((6,)),
            ],
            compiler_params=pltpu.CompilerParams(
                collective_id=0, has_side_effects=True, vmem_limit_bytes=64 * 1024 * 1024
            ),
        )(
            generator,
            hamiltonian,
            pair_weights,
            jnp.swapaxes(cross_weights, 1, 2),
            recoupling,
            jnp.transpose(cross_owner),
            tile_order,
            jnp.transpose(recoupling_index),
        )

    return jax.shard_map(
        body,
        mesh=mesh,
        in_specs=placed,
        out_specs=P(("groups", "chan"), ("tile", "rep"), None, None),
        check_vma=False,
    )
```

```python
import functools

import jax
import jax.numpy as jnp
from jax import lax
from jax.experimental import pallas as pl
from jax.experimental.pallas import tpu as pltpu
from jax.sharding import PartitionSpec as P

TS = 128
CHUNK = 32
SUB = 16
WIDE = 256
MESH = pl.DeviceIdType.MESH


def split(x):
    high = x.astype(jnp.bfloat16)
    return high, (x - high.astype(jnp.float32)).astype(jnp.bfloat16)


def store_factor(left, right, s, rows, cols, x, weights):
    high, low = split(x * weights)
    left[2 * s, rows, cols] = high
    left[2 * s + 1, rows, cols] = low
    high, low = split(x)
    right[2 * (1 - s), rows, cols] = high
    right[2 * (1 - s) + 1, rows, cols] = low


def bracket(left, right, out):
    order = out.shape[0]

    def part(c, carry):
        cols = pl.ds(pl.multiple_of(c * WIDE, WIDE), WIDE)
        total = None
        for at_left, at_right in ((0, 0), (1, 0), (0, 1), (2, 2), (3, 2), (2, 3)):
            term = jnp.dot(
                left[at_left], right[at_right, :, cols], preferred_element_type=jnp.float32
            )
            total = term if total is None else total + term
        out[:, cols] = total
        return carry

    lax.fori_loop(0, order // WIDE, part, 0)


def kernel(
    n,
    generator,
    hamiltonian,
    pair_weights_far,
    cross_weights,
    recoupling_far,
    cross_owner_far,
    tile_order_far,
    recoupling_index_far,
    out,
    generator_tiles,
    hamilton_tiles,
    pair_weights,
    recoupling,
    cross_owner,
    tile_order,
    recoupling_index,
    send,
    recv,
    weights_send,
    weights_recv,
    left,
    right,
    product,
    direct,
    back_send,
    back,
    back_turned,
    inverse,
    result,
    send_sem,
    recv_sem,
    weights_send_sem,
    weights_recv_sem,
    back_send_sem,
    back_recv_sem,
    tile_sem,
    small_sem,
):
    me = lax.axis_index("chan")
    order = generator.shape[-1]
    blocks = order // TS
    tiles = tile_order.shape[-1]
    spread = tiles // n
    chunks = TS // CHUNK
    hosted = cross_weights.shape[1]

    def partner(d):
        p, bit = me, 1
        while bit <= d:
            if d & bit:
                p = p + bit * (1 - 2 * lax.rem(lax.div(me, bit), 2))
            bit *= 2
        return p

    distances = sorted(range(1, n), key=lambda d: -d.bit_length())
    outer = jnp.logical_or(me < n // 4, me >= n - n // 4)

    def by_place(act):
        @pl.when(outer)
        def _():
            act(list(reversed(distances)))

        @pl.when(jnp.logical_not(outer))
        def _():
            act(distances)

    partners = {d: partner(d) for d in range(1, n)}

    barrier = pltpu.get_barrier_semaphore()
    for d in distances:
        pl.semaphore_signal(barrier, inc=1, device_id={"chan": partners[d]}, device_id_type=MESH)

    small_pairs = (
        (tile_order_far, tile_order),
        (cross_owner_far, cross_owner),
        (recoupling_index_far, recoupling_index),
        (cross_weights.at[0], weights_send),
        (pair_weights_far, pair_weights),
        (recoupling_far, recoupling),
    )
    fetches = [
        pltpu.make_async_copy(far, near, small_sem.at[at])
        for at, (far, near) in enumerate(small_pairs)
    ]
    fetches[0].start()
    for q in range(tiles):
        here, there = pl.ds((q // blocks) * TS, TS), pl.ds((q % blocks) * TS, TS)
        for s, (far, near) in enumerate(
            ((generator, generator_tiles), (hamiltonian, hamilton_tiles))
        ):
            fetch = pltpu.make_async_copy(
                far.at[0, 0, here, there], near.at[q], tile_sem.at[s, q]
            )
            fetch.start()
            fetches.append(fetch)
    for fetch in fetches[1 : len(small_pairs)]:
        fetch.start()
    for fetch in fetches:
        fetch.wait()
    weights_recv[me] = weights_send[...]

    def pack(ch, target, slot):
        for r in range(spread):
            q = tile_order[0, 0, target * spread + r]
            rows = pl.ds(pl.multiple_of(ch * CHUNK, CHUNK), CHUNK)
            slot[0, r] = generator_tiles[q, rows, :]
            slot[1, r] = hamilton_tiles[q, rows, :]

    def weights_copy(d, at):
        return pltpu.make_async_remote_copy(
            src_ref=weights_send,
            dst_ref=weights_recv.at[at],
            send_sem=weights_send_sem.at[d],
            recv_sem=weights_recv_sem.at[d],
            device_id={"chan": partners[d]},
            device_id_type=MESH,
        )

    def tiles_copy(ch, d, at):
        return pltpu.make_async_remote_copy(
            src_ref=send.at[ch, d],
            dst_ref=recv.at[ch, at],
            send_sem=send_sem.at[ch, d],
            recv_sem=recv_sem.at[ch, d],
            device_id={"chan": partners[d]},
            device_id_type=MESH,
        )

    def back_copy(d, at):
        return pltpu.make_async_remote_copy(
            src_ref=back_send.at[d],
            dst_ref=back.at[at],
            send_sem=back_send_sem.at[d],
            recv_sem=back_recv_sem.at[d],
            device_id={"chan": partners[d]},
            device_id_type=MESH,
        )

    def pack_partners(ch, carry):
        for d in distances:
            pack(ch, partners[d], send.at[ch, d])
        return carry

    def start_chunk(ch, carry):
        def act(ordered):
            for d in ordered:
                tiles_copy(ch, d, me).start()

        by_place(act)
        return carry

    pack_partners(0, 0)
    pl.semaphore_wait(barrier, n - 1)
    for d in distances:
        weights_copy(d, me).start()
    start_chunk(0, 0)

    def pack_and_start(ch, carry):
        pack_partners(ch, 0)
        return start_chunk(ch, carry)

    lax.fori_loop(1, chunks, pack_and_start, 0)

    def pack_own(ch, carry):
        pack(ch, me, recv.at[ch, me])
        return carry

    lax.fori_loop(0, chunks, pack_own, 0)

    pair_row = pair_weights[0]

    def split_direct(step, carry):
        a, part = lax.div(step, TS // SUB), lax.rem(step, TS // SUB)
        from_rows = pl.ds(pl.multiple_of(part * SUB, SUB), SUB)
        to_rows = pl.ds(pl.multiple_of(step * SUB, SUB), SUB)
        for b in range(blocks):
            cols = slice(b * TS, (b + 1) * TS)
            row = pair_row[:, cols]
            x, y = generator_tiles[a * blocks + b, from_rows], hamilton_tiles[a * blocks + b, from_rows]
            store_factor(left, right, 0, to_rows, cols, x, row)
            store_factor(left, right, 1, to_rows, cols, y, -row)
        return carry

    lax.fori_loop(0, order // SUB, split_direct, 0)
    bracket(left, right, product)
    for a in range(blocks):
        for b in range(blocks):
            here, there = pl.ds(a * TS, TS), pl.ds(b * TS, TS)
            direct[here, there] = 0.5 * (product[here, there] + product[there, here].T)

    def invert(q, carry):
        at = jnp.int32(0)
        for t in range(tiles):
            at = jnp.maximum(at, jnp.where(tile_order[0, 0, t] == q, t, 0))
        inverse[q] = at
        return carry

    lax.fori_loop(0, tiles, invert, 0)

    owner = cross_owner[0, me]
    slot_at = jnp.int32(0)
    for g in range(n):
        slot_at = slot_at + jnp.where(
            jnp.logical_and(g < me, cross_owner[0, g] == owner), 1, 0
        )
    slot_at = jnp.minimum(slot_at, hosted - 1)
    for d in distances:
        weights_copy(d, partners[d]).wait_recv()
    cross_row = weights_recv[owner, slot_at]
    matrix = recoupling_index[0, me]

    def mix_chunk(ch, carry):
        for d in distances:
            tiles_copy(ch, d, partners[d]).wait_recv()

        def mix(step, inner):
            s, part = lax.div(step, CHUNK // SUB), lax.rem(step, CHUNK // SUB)
            rows = pl.ds(pl.multiple_of(part * SUB, SUB), SUB)
            signed = cross_row * (1 - 2 * s).astype(jnp.float32)
            taken = [recv[ch, i % n, s, i // n, rows, :] for i in range(tiles)]
            for j in range(tiles):
                total = taken[0] * recoupling[matrix, j, 0]
                for i in range(1, tiles):
                    total = total + taken[i] * recoupling[matrix, j, i]
                start = (j // blocks) * TS + ch * CHUNK + part * SUB
                to_rows = pl.ds(pl.multiple_of(start, SUB), SUB)
                cols = slice((j % blocks) * TS, (j % blocks + 1) * TS)
                store_factor(left, right, s, to_rows, cols, total, signed[:, cols])
            return inner

        return lax.fori_loop(0, 2 * (CHUNK // SUB), mix, carry)

    lax.fori_loop(0, chunks, mix_chunk, 0)
    bracket(left, right, product)

    def mix_back(home, slot):
        def part(c, carry):
            rows = pl.ds(pl.multiple_of(c * CHUNK, CHUNK), CHUNK)
            totals = [None] * spread
            for j in range(tiles):
                start = (j // blocks) * TS + c * CHUNK
                from_rows = pl.ds(pl.multiple_of(start, CHUNK), CHUNK)
                piece = product[from_rows, (j % blocks) * TS : (j % blocks + 1) * TS]
                for r in range(spread):
                    term = piece * recoupling[matrix, j, r * n + home]
                    totals[r] = term if j == 0 else totals[r] + term
            for r in range(spread):
                slot[r, rows, :] = totals[r]
            return carry

        lax.fori_loop(0, chunks, part, 0)

    def send_back(ordered):
        for d in ordered:
            mix_back(partners[d], back_send.at[d])
            back_copy(d, me).start()

    by_place(send_back)
    mix_back(me, back.at[me])

    def turn(source):
        for r in range(spread):
            back_turned[source, r] = back[source, r].T

    turn(me)
    for d in reversed(distances):
        back_copy(d, partners[d]).wait_recv()
        turn(partners[d])

    writes = []
    for q in range(tiles):
        a, b = q // blocks, q % blocks
        at, turned_at = inverse[q], inverse[b * blocks + a]
        came = back[lax.div(at, spread), lax.rem(at, spread)]
        turned = back_turned[lax.div(turned_at, spread), lax.rem(turned_at, spread)]
        here, there = pl.ds(a * TS, TS), pl.ds(b * TS, TS)
        result[q] = direct[here, there] + 0.5 * (came + turned)
        write = pltpu.make_async_copy(result.at[q], out.at[0, 0, here, there], tile_sem.at[0, q])
        write.start()
        writes.append(write)

    for d in distances:
        weights_copy(d, me).wait_send()
        back_copy(d, me).wait_send()

    def finish(ch, carry):
        for d in distances:
            tiles_copy(ch, d, me).wait_send()
        return carry

    lax.fori_loop(0, chunks, finish, 0)
    for write in writes:
        write.wait()


def solution(mesh):
    n = mesh.shape["chan"]
    placed = (
        P(("groups", "chan"), ("tile", "rep"), None, None),
        P(("groups", "chan"), ("tile", "rep"), None, None),
        P(("groups", "chan"), ("tile", "rep"), None),
        P(("groups", "chan"), ("tile", "rep"), None, None),
        P(),
        P("groups", ("tile", "rep")),
        P(("groups", "chan"), ("tile", "rep"), None),
        P("groups", ("tile", "rep")),
    )

    def body(
        generator,
        hamiltonian,
        pair_weights,
        cross_weights,
        recoupling,
        cross_owner,
        tile_order,
        recoupling_index,
    ):
        order = generator.shape[-1]
        tiles = tile_order.shape[-1]
        spread = tiles // n
        chunks = TS // CHUNK
        hosted = cross_weights.shape[2]
        f32, bf16 = jnp.float32, jnp.bfloat16
        return pl.pallas_call(
            functools.partial(kernel, n),
            out_shape=pltpu.VMEM(generator.shape, f32),
            in_specs=[pl.BlockSpec(memory_space=pltpu.HBM)] * 8,
            out_specs=pl.BlockSpec(memory_space=pltpu.VMEM),
            scratch_shapes=[
                pltpu.VMEM((tiles, TS, TS), f32),
                pltpu.VMEM((tiles, TS, TS), f32),
                pltpu.VMEM(pair_weights.shape, f32),
                pltpu.SMEM(recoupling.shape, f32),
                pltpu.SMEM((1, n), jnp.int32),
                pltpu.SMEM(tile_order.shape, jnp.int32),
                pltpu.SMEM((1, n), jnp.int32),
                pltpu.VMEM((chunks, n, 2, spread, CHUNK, TS), f32),
                pltpu.VMEM((chunks, n, 2, spread, CHUNK, TS), f32),
                pltpu.VMEM((hosted, 1, order), f32),
                pltpu.VMEM((n, hosted, 1, order), f32),
                pltpu.VMEM((4, order, order), bf16),
                pltpu.VMEM((4, order, order), bf16),
                pltpu.VMEM((order, order), f32),
                pltpu.VMEM((order, order), f32),
                pltpu.VMEM((n, spread, TS, TS), f32),
                pltpu.VMEM((n, spread, TS, TS), f32),
                pltpu.VMEM((n, spread, TS, TS), f32),
                pltpu.SMEM((tiles,), jnp.int32),
                pltpu.VMEM((tiles, TS, TS), f32),
                pltpu.SemaphoreType.DMA((chunks, n)),
                pltpu.SemaphoreType.DMA((chunks, n)),
                pltpu.SemaphoreType.DMA((n,)),
                pltpu.SemaphoreType.DMA((n,)),
                pltpu.SemaphoreType.DMA((n,)),
                pltpu.SemaphoreType.DMA((n,)),
                pltpu.SemaphoreType.DMA((2, tiles)),
                pltpu.SemaphoreType.DMA((6,)),
            ],
            compiler_params=pltpu.CompilerParams(
                collective_id=0, has_side_effects=True, vmem_limit_bytes=56 * 1024 * 1024
            ),
        )(
            pltpu.with_memory_space_constraint(generator, pltpu.HBM),
            pltpu.with_memory_space_constraint(hamiltonian, pltpu.HBM),
            pair_weights,
            jnp.swapaxes(cross_weights, 1, 2),
            recoupling,
            jnp.transpose(cross_owner),
            tile_order,
            jnp.transpose(recoupling_index),
        )

    return jax.shard_map(
        body,
        mesh=mesh,
        in_specs=placed,
        out_specs=P(("groups", "chan"), ("tile", "rep"), None, None),
        check_vma=False,
    )
```

```python
import functools

import jax
import jax.numpy as jnp
from jax import lax
from jax.experimental import pallas as pl
from jax.experimental.pallas import tpu as pltpu
from jax.sharding import PartitionSpec as P

TS = 128
HALF = TS // 2
CHUNK = 32
SUB = 16
WIDE = 256
MESH = pl.DeviceIdType.MESH


def split(x):
    high = x.astype(jnp.bfloat16)
    return high, (x - high.astype(jnp.float32)).astype(jnp.bfloat16)


def store_factor(left, right, s, left_rows, rows, cols, x, weights):
    high, low = split(x * weights)
    left[2 * s, left_rows, cols] = high
    left[2 * s + 1, left_rows, cols] = low
    high, low = split(x)
    right[2 * (1 - s), rows, cols] = high
    right[2 * (1 - s) + 1, rows, cols] = low


def bracket(left, right, out, rows):
    order = out.shape[1]

    def part(c, carry):
        cols = pl.ds(pl.multiple_of(c * WIDE, WIDE), WIDE)
        total = None
        for at_left, at_right in ((0, 0), (1, 0), (0, 1), (2, 2), (3, 2), (2, 3)):
            term = jnp.dot(
                left[at_left, rows], right[at_right, :, cols], preferred_element_type=jnp.float32
            )
            total = term if total is None else total + term
        out[rows, cols] = total
        return carry

    lax.fori_loop(0, order // WIDE, part, 0)


def kernel(
    n,
    generator,
    hamiltonian,
    pair_weights_far,
    cross_weights,
    recoupling_far,
    cross_owner_far,
    tile_order_far,
    recoupling_index_far,
    out,
    generator_tiles,
    hamilton_tiles,
    pair_weights,
    recoupling,
    cross_owner,
    tile_order,
    recoupling_index,
    send,
    recv,
    weights_send,
    weights_recv,
    left,
    right,
    product,
    direct,
    back_send,
    back,
    back_turned,
    inverse,
    send_sem,
    recv_sem,
    weights_send_sem,
    weights_recv_sem,
    back_send_sem,
    back_recv_sem,
    tile_sem,
    small_sem,
):
    me = lax.axis_index("chan")
    order = generator.shape[-1]
    blocks = order // TS
    tiles = tile_order.shape[-1]
    spread = tiles // n
    chunks = TS // CHUNK
    hosted = cross_weights.shape[1]

    def partner(d):
        p, bit = me, 1
        while bit <= d:
            if d & bit:
                p = p + bit * (1 - 2 * lax.rem(lax.div(me, bit), 2))
            bit *= 2
        return p

    distances = sorted(range(1, n), key=lambda d: -d.bit_length())
    partners = {d: partner(d) for d in range(1, n)}

    barrier = pltpu.get_barrier_semaphore()
    for d in distances:
        pl.semaphore_signal(barrier, inc=1, device_id={"chan": partners[d]}, device_id_type=MESH)

    small_pairs = (
        (tile_order_far, tile_order),
        (cross_owner_far, cross_owner),
        (recoupling_index_far, recoupling_index),
        (cross_weights.at[0], weights_send),
        (pair_weights_far, pair_weights),
        (recoupling_far, recoupling),
    )
    fetches = [
        pltpu.make_async_copy(far, near, small_sem.at[at])
        for at, (far, near) in enumerate(small_pairs)
    ]
    fetches[0].start()
    for q in range(tiles):
        here, there = pl.ds((q // blocks) * TS, TS), pl.ds((q % blocks) * TS, TS)
        for s, (far, near) in enumerate(
            ((generator, generator_tiles), (hamiltonian, hamilton_tiles))
        ):
            fetch = pltpu.make_async_copy(
                far.at[0, 0, here, there], near.at[q], tile_sem.at[s, q]
            )
            fetch.start()
            fetches.append(fetch)
    for fetch in fetches[1 : len(small_pairs)]:
        fetch.start()
    for fetch in fetches:
        fetch.wait()
    weights_recv[me] = weights_send[...]

    def pack(ch, target, slot):
        for r in range(spread):
            q = tile_order[0, 0, target * spread + r]
            rows = pl.ds(pl.multiple_of(ch * CHUNK, CHUNK), CHUNK)
            slot[0, r] = generator_tiles[q, rows, :]
            slot[1, r] = hamilton_tiles[q, rows, :]

    def weights_copy(d, at):
        return pltpu.make_async_remote_copy(
            src_ref=weights_send,
            dst_ref=weights_recv.at[at],
            send_sem=weights_send_sem.at[d],
            recv_sem=weights_recv_sem.at[d],
            device_id={"chan": partners[d]},
            device_id_type=MESH,
        )

    def tiles_copy(ch, d, at):
        return pltpu.make_async_remote_copy(
            src_ref=send.at[ch, d],
            dst_ref=recv.at[ch, at],
            send_sem=send_sem.at[ch, d],
            recv_sem=recv_sem.at[ch, d],
            device_id={"chan": partners[d]},
            device_id_type=MESH,
        )

    def back_copy(half, d, at):
        return pltpu.make_async_remote_copy(
            src_ref=back_send.at[half, d],
            dst_ref=back.at[half, at],
            send_sem=back_send_sem.at[half, d],
            recv_sem=back_recv_sem.at[half, d],
            device_id={"chan": partners[d]},
            device_id_type=MESH,
        )

    def pack_partners(ch, carry):
        for d in distances:
            pack(ch, partners[d], send.at[ch, d])
        return carry

    def start_chunk(ch, carry):
        for d in distances:
            tiles_copy(ch, d, me).start()
        return carry

    pack_partners(0, 0)
    pl.semaphore_wait(barrier, n - 1)
    for d in distances:
        weights_copy(d, me).start()
    start_chunk(0, 0)

    def pack_and_start(ch, carry):
        pack_partners(ch, 0)
        return start_chunk(ch, carry)

    lax.fori_loop(1, chunks, pack_and_start, 0)

    def pack_own(ch, carry):
        pack(ch, me, recv.at[ch, me])
        return carry

    lax.fori_loop(0, chunks, pack_own, 0)

    pair_row = pair_weights[0]

    def split_direct(step, carry):
        a, part = lax.div(step, TS // SUB), lax.rem(step, TS // SUB)
        from_rows = pl.ds(pl.multiple_of(part * SUB, SUB), SUB)
        to_rows = pl.ds(pl.multiple_of(step * SUB, SUB), SUB)
        for b in range(blocks):
            cols = slice(b * TS, (b + 1) * TS)
            row = pair_row[:, cols]
            x, y = generator_tiles[a * blocks + b, from_rows], hamilton_tiles[a * blocks + b, from_rows]
            store_factor(left, right, 0, to_rows, to_rows, cols, x, row)
            store_factor(left, right, 1, to_rows, to_rows, cols, y, -row)
        return carry

    lax.fori_loop(0, order // SUB, split_direct, 0)
    bracket(left, right, product, slice(None))
    for a in range(blocks):
        for b in range(blocks):
            here, there = pl.ds(a * TS, TS), pl.ds(b * TS, TS)
            direct[here, there] = 0.5 * (product[here, there] + product[there, here].T)

    def invert(q, carry):
        at = jnp.int32(0)
        for t in range(tiles):
            at = jnp.maximum(at, jnp.where(tile_order[0, 0, t] == q, t, 0))
        inverse[q] = at
        return carry

    lax.fori_loop(0, tiles, invert, 0)

    owner = cross_owner[0, me]
    slot_at = jnp.int32(0)
    for g in range(n):
        slot_at = slot_at + jnp.where(
            jnp.logical_and(g < me, cross_owner[0, g] == owner), 1, 0
        )
    slot_at = jnp.minimum(slot_at, hosted - 1)
    for d in distances:
        weights_copy(d, partners[d]).wait_recv()
    cross_row = weights_recv[owner, slot_at]
    matrix = recoupling_index[0, me]

    def half_of(ch):
        return lax.div(ch, HALF // CHUNK)

    def within(ch):
        return lax.rem(ch, HALF // CHUNK) * CHUNK

    def mix_chunk(ch, carry):
        for d in distances:
            tiles_copy(ch, d, partners[d]).wait_recv()

        def mix(step, inner):
            s, part = lax.div(step, CHUNK // SUB), lax.rem(step, CHUNK // SUB)
            rows = pl.ds(pl.multiple_of(part * SUB, SUB), SUB)
            signed = cross_row * (1 - 2 * s).astype(jnp.float32)
            taken = [recv[ch, i % n, s, i // n, rows, :] for i in range(tiles)]
            for j in range(tiles):
                total = taken[0] * recoupling[matrix, j, 0]
                for i in range(1, tiles):
                    total = total + taken[i] * recoupling[matrix, j, i]
                start = half_of(ch) * (order // 2) + (j // blocks) * HALF + within(ch) + part * SUB
                left_rows = pl.ds(pl.multiple_of(start, SUB), SUB)
                start = (j // blocks) * TS + ch * CHUNK + part * SUB
                to_rows = pl.ds(pl.multiple_of(start, SUB), SUB)
                cols = slice((j % blocks) * TS, (j % blocks + 1) * TS)
                store_factor(left, right, s, left_rows, to_rows, cols, total, signed[:, cols])
            return inner

        return lax.fori_loop(0, 2 * (CHUNK // SUB), mix, carry)

    lax.fori_loop(0, chunks, mix_chunk, 0)

    def mix_back(half, home, slot):
        def part(c, carry):
            rows = pl.ds(pl.multiple_of(c * CHUNK, CHUNK), CHUNK)
            totals = [None] * spread
            for j in range(tiles):
                start = half * (order // 2) + (j // blocks) * HALF + c * CHUNK
                from_rows = pl.ds(pl.multiple_of(start, CHUNK), CHUNK)
                piece = product[from_rows, (j % blocks) * TS : (j % blocks + 1) * TS]
                for r in range(spread):
                    term = piece * recoupling[matrix, j, r * n + home]
                    totals[r] = term if j == 0 else totals[r] + term
            for r in range(spread):
                slot[r, rows, :] = totals[r]
            return carry

        lax.fori_loop(0, HALF // CHUNK, part, 0)

    for half in range(2):
        bracket(left, right, product, slice(half * (order // 2), (half + 1) * (order // 2)))
        for d in distances:
            mix_back(half, partners[d], back_send.at[half, d])
            back_copy(half, d, me).start()
    for half in range(2):
        mix_back(half, me, back.at[half, me])

    def turn(source):
        for r in range(spread):
            whole = jnp.concatenate([back[half, source, r] for half in range(2)], axis=0)
            back_turned[source, r] = whole.T

    turn(me)
    for d in reversed(distances):
        for half in range(2):
            back_copy(half, d, partners[d]).wait_recv()
        turn(partners[d])

    for q in range(tiles):
        a, b = q // blocks, q % blocks
        at, turned_at = inverse[q], inverse[b * blocks + a]
        source, r = lax.div(at, spread), lax.rem(at, spread)
        turned = back_turned[lax.div(turned_at, spread), lax.rem(turned_at, spread)]
        there = pl.ds(b * TS, TS)
        for half in range(2):
            here = pl.ds(a * TS + half * HALF, HALF)
            came = back[half, source, r]
            out[0, 0, here, there] = direct[here, there] + 0.5 * (
                came + turned[half * HALF : (half + 1) * HALF]
            )

    for d in distances:
        weights_copy(d, me).wait_send()
        for half in range(2):
            back_copy(half, d, me).wait_send()

    def finish(ch, carry):
        for d in distances:
            tiles_copy(ch, d, me).wait_send()
        return carry

    lax.fori_loop(0, chunks, finish, 0)


def solution(mesh):
    n = mesh.shape["chan"]
    placed = (
        P(("groups", "chan"), ("tile", "rep"), None, None),
        P(("groups", "chan"), ("tile", "rep"), None, None),
        P(("groups", "chan"), ("tile", "rep"), None),
        P(("groups", "chan"), ("tile", "rep"), None, None),
        P(),
        P("groups", ("tile", "rep")),
        P(("groups", "chan"), ("tile", "rep"), None),
        P("groups", ("tile", "rep")),
    )

    def body(
        generator,
        hamiltonian,
        pair_weights,
        cross_weights,
        recoupling,
        cross_owner,
        tile_order,
        recoupling_index,
    ):
        order = generator.shape[-1]
        tiles = tile_order.shape[-1]
        spread = tiles // n
        chunks = TS // CHUNK
        hosted = cross_weights.shape[2]
        f32, bf16 = jnp.float32, jnp.bfloat16
        return pl.pallas_call(
            functools.partial(kernel, n),
            out_shape=pltpu.VMEM(generator.shape, f32),
            in_specs=[pl.BlockSpec(memory_space=pltpu.HBM)] * 8,
            out_specs=pl.BlockSpec(memory_space=pltpu.VMEM),
            scratch_shapes=[
                pltpu.VMEM((tiles, TS, TS), f32),
                pltpu.VMEM((tiles, TS, TS), f32),
                pltpu.VMEM(pair_weights.shape, f32),
                pltpu.SMEM(recoupling.shape, f32),
                pltpu.SMEM((1, n), jnp.int32),
                pltpu.SMEM(tile_order.shape, jnp.int32),
                pltpu.SMEM((1, n), jnp.int32),
                pltpu.VMEM((chunks, n, 2, spread, CHUNK, TS), f32),
                pltpu.VMEM((chunks, n, 2, spread, CHUNK, TS), f32),
                pltpu.VMEM((hosted, 1, order), f32),
                pltpu.VMEM((n, hosted, 1, order), f32),
                pltpu.VMEM((4, order, order), bf16),
                pltpu.VMEM((4, order, order), bf16),
                pltpu.VMEM((order, order), f32),
                pltpu.VMEM((order, order), f32),
                pltpu.VMEM((2, n, spread, HALF, TS), f32),
                pltpu.VMEM((2, n, spread, HALF, TS), f32),
                pltpu.VMEM((n, spread, TS, TS), f32),
                pltpu.SMEM((tiles,), jnp.int32),
                pltpu.SemaphoreType.DMA((chunks, n)),
                pltpu.SemaphoreType.DMA((chunks, n)),
                pltpu.SemaphoreType.DMA((n,)),
                pltpu.SemaphoreType.DMA((n,)),
                pltpu.SemaphoreType.DMA((2, n)),
                pltpu.SemaphoreType.DMA((2, n)),
                pltpu.SemaphoreType.DMA((2, tiles)),
                pltpu.SemaphoreType.DMA((6,)),
            ],
            compiler_params=pltpu.CompilerParams(
                collective_id=0, has_side_effects=True, vmem_limit_bytes=56 * 1024 * 1024
            ),
        )(
            pltpu.with_memory_space_constraint(generator, pltpu.HBM),
            pltpu.with_memory_space_constraint(hamiltonian, pltpu.HBM),
            pair_weights,
            jnp.swapaxes(cross_weights, 1, 2),
            recoupling,
            jnp.transpose(cross_owner),
            tile_order,
            jnp.transpose(recoupling_index),
        )

    return jax.shard_map(
        body,
        mesh=mesh,
        in_specs=placed,
        out_specs=P(("groups", "chan"), ("tile", "rep"), None, None),
        check_vma=False,
    )
```

```python
import functools

import jax
import jax.numpy as jnp
from jax import lax
from jax.experimental import pallas as pl
from jax.experimental.pallas import tpu as pltpu
from jax.sharding import PartitionSpec as P

TS = 128
PARTS = 4
DEPTH = TS // PARTS
CHUNK = 32
SUB = 16
WIDE = 256
MESH = pl.DeviceIdType.MESH


def split(x):
    high = x.astype(jnp.bfloat16)
    return high, (x - high.astype(jnp.float32)).astype(jnp.bfloat16)


def store_factor(left, right, s, left_rows, rows, cols, x, weights):
    high, low = split(x * weights)
    left[2 * s, left_rows, cols] = high
    left[2 * s + 1, left_rows, cols] = low
    high, low = split(x)
    right[2 * (1 - s), rows, cols] = high
    right[2 * (1 - s) + 1, rows, cols] = low


def bracket(left, right, out, rows):
    order = out.shape[1]

    def part(c, carry):
        cols = pl.ds(pl.multiple_of(c * WIDE, WIDE), WIDE)
        total = None
        for at_left, at_right in ((0, 0), (1, 0), (0, 1), (2, 2), (3, 2), (2, 3)):
            term = jnp.dot(
                left[at_left, rows], right[at_right, :, cols], preferred_element_type=jnp.float32
            )
            total = term if total is None else total + term
        out[rows, cols] = total
        return carry

    lax.fori_loop(0, order // WIDE, part, 0)


def kernel(
    n,
    generator,
    hamiltonian,
    pair_weights_far,
    cross_weights,
    recoupling_far,
    cross_owner_far,
    tile_order_far,
    recoupling_index_far,
    out,
    generator_tiles,
    hamilton_tiles,
    pair_weights,
    recoupling,
    cross_owner,
    tile_order,
    recoupling_index,
    send,
    recv,
    weights_send,
    weights_recv,
    left,
    right,
    product,
    direct,
    back_send,
    back,
    back_turned,
    inverse,
    send_sem,
    recv_sem,
    weights_send_sem,
    weights_recv_sem,
    back_send_sem,
    back_recv_sem,
    tile_sem,
    small_sem,
):
    me = lax.axis_index("chan")
    order = generator.shape[-1]
    blocks = order // TS
    tiles = tile_order.shape[-1]
    spread = tiles // n
    chunks = TS // CHUNK
    hosted = cross_weights.shape[1]

    def partner(d):
        p, bit = me, 1
        while bit <= d:
            if d & bit:
                p = p + bit * (1 - 2 * lax.rem(lax.div(me, bit), 2))
            bit *= 2
        return p

    distances = sorted(range(1, n), key=lambda d: -d.bit_length())
    partners = {d: partner(d) for d in range(1, n)}

    barrier = pltpu.get_barrier_semaphore()
    for d in distances:
        pl.semaphore_signal(barrier, inc=1, device_id={"chan": partners[d]}, device_id_type=MESH)

    small_pairs = (
        (tile_order_far, tile_order),
        (cross_owner_far, cross_owner),
        (recoupling_index_far, recoupling_index),
        (cross_weights.at[0], weights_send),
        (pair_weights_far, pair_weights),
        (recoupling_far, recoupling),
    )
    fetches = [
        pltpu.make_async_copy(far, near, small_sem.at[at])
        for at, (far, near) in enumerate(small_pairs)
    ]
    fetches[0].start()
    for q in range(tiles):
        here, there = pl.ds((q // blocks) * TS, TS), pl.ds((q % blocks) * TS, TS)
        for s, (far, near) in enumerate(
            ((generator, generator_tiles), (hamiltonian, hamilton_tiles))
        ):
            fetch = pltpu.make_async_copy(
                far.at[0, 0, here, there], near.at[q], tile_sem.at[s, q]
            )
            fetch.start()
            fetches.append(fetch)
    for fetch in fetches[1 : len(small_pairs)]:
        fetch.start()
    later = [fetches.pop(at) for at in (5, 4, 2, 1)]
    for fetch in fetches:
        fetch.wait()
    weights_recv[me] = weights_send[...]

    def pack(ch, target, slot):
        for r in range(spread):
            q = tile_order[0, 0, target * spread + r]
            rows = pl.ds(pl.multiple_of(ch * CHUNK, CHUNK), CHUNK)
            slot[0, r] = generator_tiles[q, rows, :]
            slot[1, r] = hamilton_tiles[q, rows, :]

    def weights_copy(d, at):
        return pltpu.make_async_remote_copy(
            src_ref=weights_send,
            dst_ref=weights_recv.at[at],
            send_sem=weights_send_sem.at[d],
            recv_sem=weights_recv_sem.at[d],
            device_id={"chan": partners[d]},
            device_id_type=MESH,
        )

    def tiles_copy(ch, d, at):
        return pltpu.make_async_remote_copy(
            src_ref=send.at[ch, d],
            dst_ref=recv.at[ch, at],
            send_sem=send_sem.at[ch, d],
            recv_sem=recv_sem.at[ch, d],
            device_id={"chan": partners[d]},
            device_id_type=MESH,
        )

    def back_copy(piece_at, d, at):
        return pltpu.make_async_remote_copy(
            src_ref=back_send.at[piece_at, d],
            dst_ref=back.at[piece_at, at],
            send_sem=back_send_sem.at[piece_at, d],
            recv_sem=back_recv_sem.at[piece_at, d],
            device_id={"chan": partners[d]},
            device_id_type=MESH,
        )

    def pack_partners(ch, carry):
        for d in distances:
            pack(ch, partners[d], send.at[ch, d])
        return carry

    def start_chunk(ch, carry):
        for d in distances:
            tiles_copy(ch, d, me).start()
        return carry

    pack_partners(0, 0)
    pl.semaphore_wait(barrier, n - 1)
    for d in distances:
        weights_copy(d, me).start()
    start_chunk(0, 0)

    def pack_and_start(ch, carry):
        pack_partners(ch, 0)
        return start_chunk(ch, carry)

    lax.fori_loop(1, chunks, pack_and_start, 0)

    def pack_own(ch, carry):
        pack(ch, me, recv.at[ch, me])
        return carry

    lax.fori_loop(0, chunks, pack_own, 0)

    for fetch in later:
        fetch.wait()
    pair_row = pair_weights[0]

    def split_direct(step, carry):
        a, part = lax.div(step, TS // SUB), lax.rem(step, TS // SUB)
        from_rows = pl.ds(pl.multiple_of(part * SUB, SUB), SUB)
        to_rows = pl.ds(pl.multiple_of(step * SUB, SUB), SUB)
        for b in range(blocks):
            cols = slice(b * TS, (b + 1) * TS)
            row = pair_row[:, cols]
            x, y = generator_tiles[a * blocks + b, from_rows], hamilton_tiles[a * blocks + b, from_rows]
            store_factor(left, right, 0, to_rows, to_rows, cols, x, row)
            store_factor(left, right, 1, to_rows, to_rows, cols, y, -row)
        return carry

    lax.fori_loop(0, order // SUB, split_direct, 0)
    bracket(left, right, product, slice(None))
    for a in range(blocks):
        for b in range(blocks):
            here, there = pl.ds(a * TS, TS), pl.ds(b * TS, TS)
            direct[here, there] = 0.5 * (product[here, there] + product[there, here].T)

    def invert(q, carry):
        at = jnp.int32(0)
        for t in range(tiles):
            at = jnp.maximum(at, jnp.where(tile_order[0, 0, t] == q, t, 0))
        inverse[q] = at
        return carry

    lax.fori_loop(0, tiles, invert, 0)

    owner = cross_owner[0, me]
    slot_at = jnp.int32(0)
    for g in range(n):
        slot_at = slot_at + jnp.where(
            jnp.logical_and(g < me, cross_owner[0, g] == owner), 1, 0
        )
    slot_at = jnp.minimum(slot_at, hosted - 1)
    for d in distances:
        weights_copy(d, partners[d]).wait_recv()
    cross_row = weights_recv[owner, slot_at]
    matrix = recoupling_index[0, me]

    def part_of(ch):
        return lax.div(ch, DEPTH // CHUNK)

    def within(ch):
        return lax.rem(ch, DEPTH // CHUNK) * CHUNK

    def mix_chunk(ch, carry):
        for d in distances:
            tiles_copy(ch, d, partners[d]).wait_recv()

        def mix(step, inner):
            s, part = lax.div(step, CHUNK // SUB), lax.rem(step, CHUNK // SUB)
            rows = pl.ds(pl.multiple_of(part * SUB, SUB), SUB)
            signed = cross_row * (1 - 2 * s).astype(jnp.float32)
            taken = [recv[ch, i % n, s, i // n, rows, :] for i in range(tiles)]
            for j in range(tiles):
                total = taken[0] * recoupling[matrix, j, 0]
                for i in range(1, tiles):
                    total = total + taken[i] * recoupling[matrix, j, i]
                start = part_of(ch) * (order // PARTS) + (j // blocks) * DEPTH + within(ch) + part * SUB
                left_rows = pl.ds(pl.multiple_of(start, SUB), SUB)
                start = (j // blocks) * TS + ch * CHUNK + part * SUB
                to_rows = pl.ds(pl.multiple_of(start, SUB), SUB)
                cols = slice((j % blocks) * TS, (j % blocks + 1) * TS)
                store_factor(left, right, s, left_rows, to_rows, cols, total, signed[:, cols])
            return inner

        return lax.fori_loop(0, 2 * (CHUNK // SUB), mix, carry)

    lax.fori_loop(0, chunks, mix_chunk, 0)

    def mix_back(piece_at, home, slot):
        def part(c, carry):
            rows = pl.ds(pl.multiple_of(c * CHUNK, CHUNK), CHUNK)
            totals = [None] * spread
            for j in range(tiles):
                start = piece_at * (order // PARTS) + (j // blocks) * DEPTH + c * CHUNK
                from_rows = pl.ds(pl.multiple_of(start, CHUNK), CHUNK)
                piece = product[from_rows, (j % blocks) * TS : (j % blocks + 1) * TS]
                for r in range(spread):
                    term = piece * recoupling[matrix, j, r * n + home]
                    totals[r] = term if j == 0 else totals[r] + term
            for r in range(spread):
                slot[r, rows, :] = totals[r]
            return carry

        lax.fori_loop(0, DEPTH // CHUNK, part, 0)

    for piece_at in range(PARTS):
        bracket(left, right, product, slice(piece_at * (order // PARTS), (piece_at + 1) * (order // PARTS)))
        for d in distances:
            mix_back(piece_at, partners[d], back_send.at[piece_at, d])
            back_copy(piece_at, d, me).start()
    for piece_at in range(PARTS):
        mix_back(piece_at, me, back.at[piece_at, me])

    def turn(source):
        for r in range(spread):
            whole = jnp.concatenate([back[piece_at, source, r] for piece_at in range(PARTS)], axis=0)
            back_turned[source, r] = whole.T

    turn(me)
    for d in reversed(distances):
        for piece_at in range(PARTS):
            back_copy(piece_at, d, partners[d]).wait_recv()
        turn(partners[d])

    for q in range(tiles):
        a, b = q // blocks, q % blocks
        at, turned_at = inverse[q], inverse[b * blocks + a]
        source, r = lax.div(at, spread), lax.rem(at, spread)
        turned = back_turned[lax.div(turned_at, spread), lax.rem(turned_at, spread)]
        there = pl.ds(b * TS, TS)
        for piece_at in range(PARTS):
            here = pl.ds(a * TS + piece_at * DEPTH, DEPTH)
            came = back[piece_at, source, r]
            out[0, 0, here, there] = direct[here, there] + 0.5 * (
                came + turned[piece_at * DEPTH : (piece_at + 1) * DEPTH]
            )

    for d in distances:
        weights_copy(d, me).wait_send()
        for piece_at in range(PARTS):
            back_copy(piece_at, d, me).wait_send()

    def finish(ch, carry):
        for d in distances:
            tiles_copy(ch, d, me).wait_send()
        return carry

    lax.fori_loop(0, chunks, finish, 0)


def solution(mesh):
    n = mesh.shape["chan"]
    placed = (
        P(("groups", "chan"), ("tile", "rep"), None, None),
        P(("groups", "chan"), ("tile", "rep"), None, None),
        P(("groups", "chan"), ("tile", "rep"), None),
        P(("groups", "chan"), ("tile", "rep"), None, None),
        P(),
        P("groups", ("tile", "rep")),
        P(("groups", "chan"), ("tile", "rep"), None),
        P("groups", ("tile", "rep")),
    )

    def body(
        generator,
        hamiltonian,
        pair_weights,
        cross_weights,
        recoupling,
        cross_owner,
        tile_order,
        recoupling_index,
    ):
        order = generator.shape[-1]
        tiles = tile_order.shape[-1]
        spread = tiles // n
        chunks = TS // CHUNK
        hosted = cross_weights.shape[2]
        f32, bf16 = jnp.float32, jnp.bfloat16
        return pl.pallas_call(
            functools.partial(kernel, n),
            out_shape=pltpu.VMEM(generator.shape, f32),
            in_specs=[pl.BlockSpec(memory_space=pltpu.HBM)] * 8,
            out_specs=pl.BlockSpec(memory_space=pltpu.VMEM),
            scratch_shapes=[
                pltpu.VMEM((tiles, TS, TS), f32),
                pltpu.VMEM((tiles, TS, TS), f32),
                pltpu.VMEM(pair_weights.shape, f32),
                pltpu.SMEM(recoupling.shape, f32),
                pltpu.SMEM((1, n), jnp.int32),
                pltpu.SMEM(tile_order.shape, jnp.int32),
                pltpu.SMEM((1, n), jnp.int32),
                pltpu.VMEM((chunks, n, 2, spread, CHUNK, TS), f32),
                pltpu.VMEM((chunks, n, 2, spread, CHUNK, TS), f32),
                pltpu.VMEM((hosted, 1, order), f32),
                pltpu.VMEM((n, hosted, 1, order), f32),
                pltpu.VMEM((4, order, order), bf16),
                pltpu.VMEM((4, order, order), bf16),
                pltpu.VMEM((order, order), f32),
                pltpu.VMEM((order, order), f32),
                pltpu.VMEM((PARTS, n, spread, DEPTH, TS), f32),
                pltpu.VMEM((PARTS, n, spread, DEPTH, TS), f32),
                pltpu.VMEM((n, spread, TS, TS), f32),
                pltpu.SMEM((tiles,), jnp.int32),
                pltpu.SemaphoreType.DMA((chunks, n)),
                pltpu.SemaphoreType.DMA((chunks, n)),
                pltpu.SemaphoreType.DMA((n,)),
                pltpu.SemaphoreType.DMA((n,)),
                pltpu.SemaphoreType.DMA((PARTS, n)),
                pltpu.SemaphoreType.DMA((PARTS, n)),
                pltpu.SemaphoreType.DMA((2, tiles)),
                pltpu.SemaphoreType.DMA((6,)),
            ],
            compiler_params=pltpu.CompilerParams(
                collective_id=0, has_side_effects=True, vmem_limit_bytes=56 * 1024 * 1024
            ),
        )(
            pltpu.with_memory_space_constraint(generator, pltpu.HBM),
            pltpu.with_memory_space_constraint(hamiltonian, pltpu.HBM),
            pair_weights,
            jnp.swapaxes(cross_weights, 1, 2),
            recoupling,
            jnp.transpose(cross_owner),
            tile_order,
            jnp.transpose(recoupling_index),
        )

    return jax.shard_map(
        body,
        mesh=mesh,
        in_specs=placed,
        out_specs=P(("groups", "chan"), ("tile", "rep"), None, None),
        check_vma=False,
    )
```
